32 devices in a mesh: ctx: 16 (over z, y, x), head: 2 (over core).
Axes of the slice: x: 2, y: 2, z: 4, core: 2. Of those that a mesh axis runs over, the one named last changes fastest.
Arguments:
- tokens: bfloat16 [4096, 2048], P('ctx'), may hold values from -6 to 6
- queries: float32 [4096, 256], P('ctx', 'head'), may hold values from -6 to 6
- values: float32 [4096, 256], P('ctx', 'head'), may hold values from -6 to 6
- dout: float32 [4096, 256], P('ctx', 'head'), may hold values from -6 to 6
- key_weight: bfloat16 [2048, 4, 256], P('ctx', None, 'head'), may hold values from -0.125 to 0.125
- routing: int32 [4096, 2], P('ctx'), may hold values from 0 to 3, all different within a row
- gates: float32 [4096, 2], P('ctx'), may hold values from 0.25 to 1
Outputs:
- key_grad: float32 [2048, 4, 256], P('ctx', None, 'head')
- query_grad: float32 [4096, 256], P('ctx', 'head')
- value_grad: float32 [4096, 256], P('ctx', 'head')
- gate_grad: float32 [4096, 2], P('ctx')
The draws below stay inside these ranges and needn't reach their ends.
Inputs may be any that keep to these rules, and one draw needn't show every extreme that they name: `routing`: each row names 2 different memories.
All inputs are finite; a program needn't handle non-finite values.
Results may differ from the reference program's by a relative error of at most 0.0029.
Values may be sent and summed in bfloat16 or wider, within the bound.
No kernel may reach another device: no remote copies, remote signals or barrier semaphores. Data moves between devices by JAX's collectives and lax.ppermute only.
A program may use at most 128 MiB of HBM per device.

```python
import math
import jax
import jax.numpy as jnp
from jax import lax

D = 2048
HD = 128
MEM = 4
TOP = 2
TOK_DEV = 256
HW = 256
TOKENS = 4096


def spiked(result, rng, source, target, parts, factor):
    def block_of(axis_at):
        return (jnp.arange(result.shape[axis_at]) // (result.shape[axis_at] // parts)).reshape((-1,) + (1,) * (result.ndim - 1 - axis_at))

    first = jax.random.permutation(rng, parts)[block_of(target)]
    other_side = (block_of(target) + parts // 2) % parts
    return jnp.where((block_of(source) == first) | (block_of(source) == other_side), factor * result, result)


def block_scale(rng, shape, pieces, least, top_value):
    def one(dim, shards_of):
        heights = jax.random.uniform(jax.random.fold_in(jax.random.fold_in(rng, 6), dim), (shards_of,), jnp.float32, least / len(pieces), top_value / len(pieces))
        return jnp.repeat(jnp.exp(heights), shape[dim] // shards_of).reshape((-1,) + (1,) * (len(shape) - dim - 1))

    gain = one(*pieces[0])
    for cut in pieces[1:]:
        gain = gain * one(*cut)
    return gain


def choose_distinct(stream_key, rows, number_of, top, lift):
    sequence = jax.random.permutation(jax.random.fold_in(stream_key, 1), number_of)
    boost = sequence
    for power in range(3):
        boost = boost * boost // number_of
    boost = boost * lift // number_of
    tickets = jax.random.randint(jax.random.fold_in(stream_key, 2), (rows, number_of), 0, 4096) + boost
    holders = jax.random.permutation(jax.random.fold_in(stream_key, 3), rows)[jnp.arange(number_of) % rows]
    tickets = jnp.where(jnp.arange(rows)[:, None] == holders[None, :], 1 << 14, tickets)
    priority = tickets * number_of + jnp.arange(number_of)
    return lax.top_k(priority.astype(jnp.int32), top)[1].astype(jnp.int32)


def gaussian(own_key, dims, deviation, bound, shards=(), held_as=jnp.bfloat16):
    gain = block_scale(own_key, dims, shards, -0.22, 0.18) if shards else 1.0
    result = jax.random.normal(own_key, dims, jnp.float32) * deviation * gain
    return jnp.minimum(jnp.maximum(result, -bound), bound).astype(held_as)


def gaussian_with(rng, dims, spread, reach, cuts, heavy, kind=jnp.bfloat16):
    array = spread * jax.random.normal(rng, dims, jnp.float32)
    if cuts:
        array = array * block_scale(rng, dims, cuts, -0.22, 0.18)
    return jnp.clip(spiked(array, jax.random.fold_in(rng, 3), *heavy), -reach, reach).astype(kind)


def setup_inputs(seed: int = 0) -> dict:
    seeds = jax.random.split(jax.random.key(seed), 8)
    return {
        "tokens": gaussian_with(seeds[0], (TOKENS, D), 1.0, 6.0, ((0, 16),), (0, 1, 16, 2.0)),
        "queries": gaussian(seeds[1], (TOKENS, HW), 1.0, 6.0, ((0, 16), (1, 2)), jnp.float32),
        "values": gaussian(seeds[2], (TOKENS, HW), 1.0, 6.0, ((0, 16), (1, 2)), jnp.float32),
        "dout": gaussian(seeds[3], (TOKENS, HW), 1.0, 6.0, ((0, 16), (1, 2)), jnp.float32),
        "key_weight": gaussian(seeds[4], (D, MEM, HW), D ** -0.5, 0.125, ((0, 16), (2, 2))),
        "routing": choose_distinct(seeds[5], TOKENS, MEM, TOP, 4096),
        "gates": jnp.clip(0.25 + 0.75 * jax.random.uniform(seeds[6], (TOKENS, TOP), jnp.float32) ** block_scale(seeds[6], (TOKENS, TOP), ((0, 16),), -0.2, 0.2), 0.25, 1.0),
    }


def routing_tables(routing, gates, memories):
    onehot = (routing[:, :, None] == jnp.arange(memories, dtype=jnp.int32)[None, None, :]).astype(jnp.float32)
    routed = lax.optimization_barrier(jnp.sum(onehot, axis=1))
    weighted = lax.optimization_barrier(jnp.sum(gates[:, :, None] * onehot, axis=1))
    return (routed, weighted, onehot)

def block_states(queries, values, dout, keys, routed, weighted, scale):
    highest = lax.Precision.HIGHEST
    masked_keys = keys * routed[:, :, None]
    key_local = jnp.einsum('tmk,tv->mkv', masked_keys, values, precision=highest)
    lifted = weighted[:, :, None] * queries[:, None, :]
    grad_local = scale * jnp.einsum('tmk,tv->mkv', lifted, dout, precision=highest)
    return (key_local, grad_local)

def block_grads(queries, values, dout, keys, routed, weighted, key_in, grad_in, scale):
    highest = lax.Precision.HIGHEST
    count = queries.shape[0]
    memories = keys.shape[1]
    head_dim = keys.shape[2]
    places = jnp.arange(count, dtype=jnp.int32)
    causal = (places[:, None] >= places[None, :]).astype(jnp.float32)
    masked_keys = keys * routed[:, :, None]
    scores = jnp.dot(dout, values.T, precision=highest) * causal
    carried_q = jnp.einsum('tv,mkv->tmk', dout, key_in, precision=highest)
    inner_q = jnp.dot(scores, masked_keys.reshape(count, memories * head_dim), precision=highest).reshape(count, memories, head_dim)
    state_dout = carried_q + inner_q
    query_grad = scale * jnp.einsum('tm,tmk->tk', weighted, state_dout, precision=highest)
    gate_part = scale * jnp.einsum('tk,tmk->tm', queries, state_dout, precision=highest)
    lifted = (weighted[:, :, None] * queries[:, None, :]).reshape(count, memories * head_dim)
    carried_k = jnp.einsum('tv,mkv->tmk', values, grad_in, precision=highest)
    inner_k = scale * jnp.dot(scores.T, lifted, precision=highest).reshape(count, memories, head_dim)
    key_part = routed[:, :, None] * (carried_k + inner_k)
    carried_v = jnp.einsum('tmk,mkv->tv', masked_keys, grad_in, precision=highest)
    products = jnp.einsum('sk,tmk->mst', queries, masked_keys, precision=highest)
    mixed = jnp.einsum('mst,sm->st', products, weighted, precision=highest) * causal
    value_grad = carried_v + scale * jnp.dot(mixed.T, dout, precision=highest)
    return (query_grad, key_part, value_grad, gate_part)

def reference(tokens, queries, values, dout, key_weight, routing, gates):
    total = tokens.shape[0]
    width = tokens.shape[1]
    memories = key_weight.shape[1]
    heads = queries.shape[1] // HD
    blocks = total // TOK_DEV
    scale = 1.0 / math.sqrt(HD * TOKENS)
    routed, weighted, onehot = routing_tables(routing, gates, memories)
    routed_blocks = routed.reshape(blocks, TOK_DEV, memories)
    weighted_blocks = weighted.reshape(blocks, TOK_DEV, memories)

    def per_head(inputs):
        head_queries, head_values, head_dout, head_weight = inputs
        keys = jnp.dot(tokens, head_weight.reshape(width, memories * HD), preferred_element_type=jnp.float32)
        keys_blocks = keys.reshape(blocks, TOK_DEV, memories, HD)
        query_blocks = head_queries.reshape(blocks, TOK_DEV, HD)
        value_blocks = head_values.reshape(blocks, TOK_DEV, HD)
        dout_blocks = head_dout.reshape(blocks, TOK_DEV, HD)
        states_fn = jax.vmap(lambda q, v, d, k, r, w: block_states(q, v, d, k, r, w, scale))
        key_local, grad_local = states_fn(query_blocks, value_blocks, dout_blocks, keys_blocks, routed_blocks, weighted_blocks)
        key_in = jnp.cumsum(key_local, axis=0) - key_local
        grad_in = lax.optimization_barrier(jnp.sum(grad_local, axis=0)) - jnp.cumsum(grad_local, axis=0)
        grads_fn = jax.vmap(lambda q, v, d, k, r, w, a, b: block_grads(q, v, d, k, r, w, a, b, scale))
        query_grad, key_part, value_grad, gate_part = grads_fn(query_blocks, value_blocks, dout_blocks, keys_blocks, routed_blocks, weighted_blocks, key_in, grad_in)
        key_low = key_part.reshape(total, memories * HD).astype(jnp.bfloat16)
        weight_grad = lax.dot_general(tokens, key_low, (((0,), (0,)), ((), ())), preferred_element_type=jnp.float32)
        return (query_grad.reshape(total, HD), value_grad.reshape(total, HD), weight_grad.reshape(width, memories, HD), gate_part.reshape(total, memories))
    query_heads = queries.reshape(total, heads, HD).transpose(1, 0, 2)
    value_heads = values.reshape(total, heads, HD).transpose(1, 0, 2)
    dout_heads = dout.reshape(total, heads, HD).transpose(1, 0, 2)
    weight_heads = key_weight.reshape(width, memories, heads, HD).transpose(2, 0, 1, 3)
    query_all, value_all, weight_all, gate_all = lax.map(per_head, (query_heads, value_heads, dout_heads, weight_heads))
    query_grad = query_all.transpose(1, 0, 2).reshape(total, heads * HD)
    value_grad = value_all.transpose(1, 0, 2).reshape(total, heads * HD)
    key_grad = weight_all.transpose(1, 2, 0, 3).reshape(width, memories, heads * HD)
    gate_sum = lax.optimization_barrier(jnp.sum(gate_all, axis=0))
    gate_grad = jnp.einsum('tjm,tm->tj', onehot, gate_sum, precision=lax.Precision.HIGHEST)
    return (key_grad, query_grad, value_grad, gate_grad)
```

```python
import functools
import math

import jax
import jax.numpy as jnp
from jax import lax
from jax.experimental import pallas as pl
from jax.experimental.pallas import tpu as pltpu
from jax.sharding import PartitionSpec as P

F32 = jnp.float32
BF16 = jnp.bfloat16


def split(x):
    high = x.astype(BF16)
    return high, (x - high.astype(F32)).astype(BF16)


def dot3(a, b, b_last=False):
    dims = (((1,), (1 if b_last else 0,)), ((), ()))

    def one(x, y):
        return lax.dot_general(x, y, dims, preferred_element_type=F32)

    return one(a[0], b[0]) + (one(a[0], b[1]) + one(a[1], b[0]))


def routed_columns(routing, memories):
    columns = []
    for m in range(memories):
        hit = (routing == m).astype(F32)
        columns.append(jnp.sum(hit, axis=1, keepdims=True))
    return columns


def weighted_columns(routing, gates, memories):
    return [
        jnp.sum(jnp.where(routing == m, gates, 0.0), axis=1, keepdims=True) for m in range(memories)
    ]


def lift(queries, routing, gates, memories):
    return jnp.concatenate(
        [w * queries for w in weighted_columns(routing, gates, memories)], axis=1
    )


def mask(x, routing, memories):
    width = x.shape[1] // memories
    return jnp.concatenate(
        [r * x[:, m * width : (m + 1) * width] for m, r in enumerate(routed_columns(routing, memories))],
        axis=1,
    )


def call(body, outs, *args, scratch=(), spaces=None, flops=0):
    vmem = pl.BlockSpec(memory_space=pltpu.VMEM)
    size = sum(a.size * a.dtype.itemsize for a in args)
    return pl.pallas_call(
        body,
        out_shape=outs,
        in_specs=[vmem] * len(args) if spaces is None else spaces,
        out_specs=jax.tree.map(lambda _: vmem, outs),
        scratch_shapes=list(scratch),
        cost_estimate=pl.CostEstimate(flops=flops, bytes_accessed=size, transcendentals=0),
        compiler_params=pltpu.CompilerParams(vmem_limit_bytes=40 * 1024 * 1024),
    )(*args)


def grad_states(memories, scale, q_ref, dout_ref, routing_ref, gates_ref, a_ref, b_ref):
    lifted = lift(q_ref[...], routing_ref[...], gates_ref[...], memories)
    states = scale * dot3(split(dout_ref[...].T), split(lifted))
    half = a_ref.shape[1]
    a_ref[...] = states[:, :half]
    b_ref[...] = states[:, half:]


def inner_key(memories, scale, q_ref, v_ref, dout_ref, routing_ref, gates_ref, out_ref):
    count = q_ref.shape[0]
    routing = routing_ref[...]
    lifted = lift(q_ref[...], routing, gates_ref[...], memories)
    places = lax.broadcasted_iota(jnp.int32, (count, count), 0)
    later = lax.broadcasted_iota(jnp.int32, (count, count), 1)
    scores = dot3(split(v_ref[...]), split(dout_ref[...]), True)
    scores = jnp.where(later >= places, scores, 0.0)
    out_ref[...] = scale * dot3(split(scores), split(lifted))


def turned_tokens(parts, here_ref, tokens_ref, out_ref, turned):
    width = tokens_ref.shape[1]
    step = 256
    for at in range(0, width, step):
        turned[at : at + step, :] = tokens_ref[:, at : at + step].T
    rows = width // parts
    here = here_ref[0]
    for off in range(parts):
        start = pl.multiple_of((here ^ off) * rows, rows)
        out_ref[off * rows : (off + 1) * rows, :] = turned[pl.ds(start, rows), :]


def key_states(memories, layout, parts, here_ref, *refs):
    chunks = len(layout)
    chunk_refs = refs[:chunks]
    tokens_ref, v_ref, routing_ref, keys_ref, a_ref, b_ref, weights, sem = refs[chunks:]
    rows = weights.shape[0] // parts
    here = here_ref[0]
    copies = []
    for ref, (column, source, blocks) in zip(chunk_refs, layout, strict=True):
        half = a_ref.shape[1]
        for k, off in enumerate(blocks):
            start = pl.multiple_of((here ^ off) * rows, rows)
            copy = pltpu.make_async_copy(
                ref.at[pl.ds(k * rows, rows), pl.ds(source * half, half)],
                weights.at[pl.ds(start, rows), pl.ds(column * half, half)],
                sem.at[len(copies)],
            )
            copy.start()
            copies.append(copy)
    for copy in copies:
        copy.wait()
    keys = jnp.dot(tokens_ref[...], weights[...], preferred_element_type=F32)
    keys = mask(keys, routing_ref[...], memories)
    keys_ref[...] = keys
    states = dot3(split(v_ref[...].T), split(keys))
    half = a_ref.shape[1]
    a_ref[...] = states[:, :half]
    b_ref[...] = states[:, half:]


def inner_rest(memories, scale, q_ref, v_ref, dout_ref, routing_ref, gates_ref, keys_ref, value_ref, state_ref):
    count = q_ref.shape[0]
    places = lax.broadcasted_iota(jnp.int32, (count, count), 0)
    others = lax.broadcasted_iota(jnp.int32, (count, count), 1)
    keys = split(keys_ref[...])
    dout = split(dout_ref[...])
    lifted = lift(q_ref[...], routing_ref[...], gates_ref[...], memories)
    mixed = jnp.where(others >= places, dot3(keys, split(lifted), True), 0.0)
    value_ref[...] = scale * dot3(split(mixed), dout)
    scores = jnp.where(places >= others, dot3(dout, split(v_ref[...]), True), 0.0)
    state_ref[...] = dot3(split(scores), keys)


def key_grad_low(memories, v_ref, routing_ref, inner_ref, grad_a, grad_b):
    values = split(v_ref[...])
    carried = jnp.concatenate([dot3(values, split(grad_a)), dot3(values, split(grad_b))], axis=1)
    return mask(carried + inner_ref[...], routing_ref[...], memories).astype(BF16)


def blocks_of(order, chosen, parts):
    found = []
    for place in range(parts):
        off = 0
        for k, bit in enumerate(order):
            if place >> (len(order) - 1 - k) & 1:
                off |= 1 << bit
        if (off >> order[0]) & 1 == chosen:
            found.append(off)
    return found


def products(turned_ref, low, parts, orders, chosen, out_refs):
    rows = turned_ref.shape[0] // parts
    half = low.shape[1] // 2
    for h, (order, out_ref) in enumerate(zip(orders, out_refs, strict=True)):
        side = low[:, h * half : (h + 1) * half]
        for k, off in enumerate(blocks_of(order, chosen, parts)):
            block = turned_ref[off * rows : (off + 1) * rows, :]
            out_ref[k * rows : (k + 1) * rows, :] = jnp.dot(
                block, side, preferred_element_type=F32
            ).astype(out_ref.dtype)


def key_sent(memories, parts, orders, v_ref, routing_ref, inner_ref, ga_ref, gb_ref, turned_ref, low_ref, a_ref, b_ref):
    low = key_grad_low(memories, v_ref, routing_ref, inner_ref, ga_ref[...], gb_ref[...])
    low_ref[...] = low
    products(turned_ref, low, parts, orders, 1, (a_ref, b_ref))


def key_kept(parts, orders, low_ref, turned_ref, a_ref, b_ref):
    products(turned_ref, low_ref[...], parts, orders, 0, (a_ref, b_ref))


def value_out(inner_ref, keys_ref, ga_ref, gb_ref, out_ref):
    half = ga_ref.shape[1]
    keys = split(keys_ref[...])
    first = dot3((keys[0][:, :half], keys[1][:, :half]), split(ga_ref[...]), True)
    second = dot3((keys[0][:, half:], keys[1][:, half:]), split(gb_ref[...]), True)
    out_ref[...] = inner_ref[...] + (first + second)


def query_out(memories, scale, q_ref, dout_ref, routing_ref, gates_ref, state_ref, sa_ref, sb_ref, query_ref, gate_ref):
    dout = split(dout_ref[...])
    state = state_ref[...] + jnp.concatenate(
        [dot3(dout, split(sa_ref[...])), dot3(dout, split(sb_ref[...]))], axis=1
    )
    queries = q_ref[...]
    routing = routing_ref[...]
    width = queries.shape[1]
    query = jnp.zeros_like(queries)
    gate = jnp.zeros(gate_ref.shape, F32)
    for m, w in enumerate(weighted_columns(routing, gates_ref[...], memories)):
        part = state[:, m * width : (m + 1) * width]
        query = query + w * part
        mine = jnp.sum(queries * part, axis=1, keepdims=True)
        gate = gate + jnp.where(routing == m, mine, 0.0)
    query_ref[...] = scale * query
    gate_ref[...] = scale * gate


def swap(x, bit, parts):
    return lax.ppermute(x, "ctx", [(i, i ^ (1 << bit)) for i in range(parts)])


def one_way(x, bit, parts, reverse):
    sources = [i for i in range(parts) if (i >> bit & 1) == (1 if reverse else 0)]
    return lax.ppermute(x, "ctx", [(i, i ^ (1 << bit)) for i in sources])


def prefix(state, bits, parts, here, reverse, wire):
    total = state
    before = jnp.zeros_like(state)
    for bit in bits:
        if bit == bits[-1]:
            return before + one_way(total.astype(wire), bit, parts, reverse).astype(F32)
        got = swap(total.astype(wire), bit, parts).astype(F32)
        after = (here >> bit & 1) == (0 if reverse else 1)
        before = before + jnp.where(after, got, 0.0)
        total = total + got
    return before


def prefix_x_last(state, bits, parts, here, reverse, wire):
    low, second, high = bits[0], bits[1], bits[2:]
    own = state
    got = swap(own.astype(wire), second, parts).astype(F32)
    after = (here >> second & 1) == (0 if reverse else 1)
    before = prefix(own + got, high, parts, here, reverse, wire) + jnp.where(after, got, 0.0)
    first = (here >> low & 1) == (1 if reverse else 0)
    sent = before + jnp.where(first, own, 0.0)
    return before + swap(sent.astype(wire), low, parts).astype(F32)


def reduce_scatter(kept, got, order, parts):
    for bit in order[1:]:
        rows = kept.shape[0] // 2
        sent = (kept[rows:] + got[rows:].astype(F32)).astype(BF16)
        kept = kept[:rows] + got[:rows].astype(F32)
        got = swap(sent, bit, parts)
    return kept + got.astype(F32)


def on_device(tokens, queries, values, dout, key_weight, routing, gates):
    count, width = tokens.shape
    rows, memories, head_dim = key_weight.shape
    parts = lax.axis_size("ctx")
    bits = list(range(parts.bit_length() - 1))
    here = lax.axis_index("ctx")
    at = here.astype(jnp.int32).reshape(1)
    scale = 1.0 / math.sqrt(head_dim * count * parts)
    full = memories * head_dim
    half = full // 2
    smem = pl.BlockSpec(memory_space=pltpu.SMEM)
    vmem = pl.BlockSpec(memory_space=pltpu.VMEM)
    anywhere = pl.BlockSpec(memory_space=pl.ANY)

    def shape(r, c, dtype=F32):
        return jax.ShapeDtypeStruct((r, c), dtype)

    gathered = key_weight.reshape(rows, full)
    blocks = [0]
    for bit in bits[2:]:
        gathered = jnp.concatenate([gathered, swap(gathered, bit, parts)], axis=0)
        blocks = blocks + [off | (1 << bit) for off in blocks]

    grad_a, grad_b = call(
        functools.partial(grad_states, memories, scale),
        (shape(head_dim, half), shape(head_dim, half)),
        queries, dout, routing, gates,
        flops=6 * count * head_dim * full,
    )
    grad_in_a = prefix(grad_a, bits, parts, here, True, F32)
    grad_in_b = prefix_x_last(grad_b, bits, parts, here, True, F32)

    chunks = [gathered, gathered]
    layout = [(0, 0, blocks), (1, 1, blocks)]
    for side in range(2):
        first, second = (bits[1], bits[0]) if side == 0 else (bits[0], bits[1])
        mine = gathered[:, side * half : (side + 1) * half]
        near = swap(mine, first, parts)
        far = swap(mine, second, parts)
        both = swap(near, second, parts)
        chunks += [near, far, both]
        one, two = 1 << first, 1 << second
        layout += [
            (side, 0, [off | one for off in blocks]),
            (side, 0, [off | two for off in blocks]),
            (side, 0, [off | one | two for off in blocks]),
        ]

    inner_k = call(
        functools.partial(inner_key, memories, scale),
        shape(count, full),
        queries, values, dout, routing, gates,
        flops=6 * count * count * (head_dim + full),
    )
    turned = call(
        functools.partial(turned_tokens, parts),
        shape(width, count, BF16),
        at, tokens,
        spaces=[smem, vmem],
        scratch=[pltpu.VMEM((width, count), BF16)],
        flops=2 * width * count,
    )

    orders = (bits, [bits[1], bits[0]] + bits[2:])
    low, sent_a, sent_b = call(
        functools.partial(key_sent, memories, parts, orders),
        (shape(count, full, BF16), shape(width // 2, half, BF16), shape(width // 2, half, BF16)),
        values, routing, inner_k, grad_in_a, grad_in_b, turned,
        flops=count * width * full + 6 * count * head_dim * full,
    )
    got_a = swap(sent_a, orders[0][0], parts)
    got_b = swap(sent_b, orders[1][0], parts)
    kept_a, kept_b = call(
        functools.partial(key_kept, parts, orders),
        (shape(width // 2, half), shape(width // 2, half)),
        low, turned,
        flops=count * width * full,
    )
    key_grad_a = reduce_scatter(kept_a, got_a, orders[0], parts)
    key_grad_b = reduce_scatter(kept_b, got_b, orders[1], parts)
    key_grad = jnp.concatenate([key_grad_a, key_grad_b], axis=1).reshape(rows, memories, head_dim)

    keys, state_a, state_b = call(
        functools.partial(key_states, memories, layout, parts),
        (shape(count, full), shape(head_dim, half), shape(head_dim, half)),
        at, *chunks, tokens, values, routing,
        spaces=[smem] + [anywhere] * len(chunks) + [vmem] * 3,
        scratch=[
            pltpu.VMEM((width, full), BF16),
            pltpu.SemaphoreType.DMA((sum(len(entry[2]) for entry in layout),)),
        ],
        flops=2 * count * width * full + 6 * count * head_dim * full,
    )
    state_in_a = prefix(state_a, bits, parts, here, False, BF16)
    state_in_b = prefix_x_last(state_b, bits, parts, here, False, BF16)
    inner_v, inner_state = call(
        functools.partial(inner_rest, memories, scale),
        (shape(count, head_dim), shape(count, full)),
        queries, values, dout, routing, gates, keys,
        flops=12 * count * count * (head_dim + full),
    )
    value_grad = call(
        value_out,
        shape(count, head_dim),
        inner_v, keys, grad_in_a, grad_in_b,
        flops=6 * count * head_dim * full,
    )
    query_grad, gate_part = call(
        functools.partial(query_out, memories, scale),
        (shape(count, head_dim), shape(count, routing.shape[1])),
        queries, dout, routing, gates, inner_state, state_in_a, state_in_b,
        flops=6 * count * head_dim * full,
    )
    gate_grad = lax.psum(gate_part, "head")
    return (key_grad, query_grad, value_grad, gate_grad)


def solution(mesh):
    return jax.shard_map(
        on_device,
        mesh=mesh,
        in_specs=(
            P("ctx", None),
            P("ctx", "head"),
            P("ctx", "head"),
            P("ctx", "head"),
            P("ctx", None, "head"),
            P("ctx", None),
            P("ctx", None),
        ),
        out_specs=(P("ctx", None, "head"), P("ctx", "head"), P("ctx", "head"), P("ctx", None)),
        check_vma=False,
    )
```

```python
import functools
import math

import jax
import jax.numpy as jnp
from jax import lax
from jax.experimental import pallas as pl
from jax.experimental.pallas import tpu as pltpu
from jax.sharding import PartitionSpec as P

F32 = jnp.float32
BF16 = jnp.bfloat16
F16 = jnp.float16
GROUP = 4
TAIL = 16


def split(x):
    high = x.astype(BF16)
    return high, (x - high.astype(F32)).astype(BF16)


def dot3(a, b, b_last=False):
    dims = (((1,), (1 if b_last else 0,)), ((), ()))

    def one(x, y):
        return lax.dot_general(x, y, dims, preferred_element_type=F32)

    return one(a[0], b[0]) + (one(a[0], b[1]) + one(a[1], b[0]))


def part(x, k, width):
    return x[:, k * width : (k + 1) * width]


def call(body, outs, *args, scratch=(), spaces=None, flops=0):
    vmem = pl.BlockSpec(memory_space=pltpu.VMEM)
    size = sum(a.size * a.dtype.itemsize for a in args)
    return pl.pallas_call(
        body,
        out_shape=outs,
        in_specs=[vmem] * len(args) if spaces is None else spaces,
        out_specs=jax.tree.map(lambda _: vmem, outs),
        scratch_shapes=list(scratch),
        cost_estimate=pl.CostEstimate(flops=flops, bytes_accessed=size, transcendentals=0),
        compiler_params=pltpu.CompilerParams(vmem_limit_bytes=40 * 1024 * 1024),
    )(*args)


def exponent(x):
    top = jnp.max(jnp.abs(x), axis=(0, 1), keepdims=True)
    return jnp.clip(jnp.ceil(jnp.log(jnp.maximum(top, 1e-30)) * (1.0 / math.log(2.0))), -90.0, 40.0) - 14.0


def power(k):
    return jnp.exp(k * math.log(2.0))


def messages(place_ref, q_ref, v_ref, dout_ref, routing_ref, gates_ref, own, near, far, both):
    count, width = q_ref.shape
    routing, gates = routing_ref[...], gates_ref[...]
    place = place_ref[0]
    q, v, dout = q_ref[...], v_ref[...], dout_ref[...]
    exponents = [exponent(x) for x in (q, v, dout)]
    scales = [1.0 / power(k) for k in exponents]
    for off, ref in enumerate((own, near, far, both)):
        hit = routing == (place ^ off)
        weight = jnp.sum(jnp.where(hit, gates, 0.0), axis=1, keepdims=True)
        routed = jnp.sum(hit.astype(F32), axis=1, keepdims=True)
        for k, x in enumerate((weight * q, routed * v, dout)):
            column = slice(k * width, (k + 1) * width)
            if off:
                ref[:count, column] = x * scales[k]
                ref[count:, column] = jnp.broadcast_to(exponents[k], (TAIL, width))
            else:
                ref[:, column] = x


def group_sums(place, states, sums_ref, total_ref, reverse):
    size = states[0].shape[0]
    for to in range(GROUP):
        total = jnp.zeros_like(states[0])
        for off in range(GROUP):
            counts = (place ^ off) > (place ^ to) if reverse else (place ^ off) < (place ^ to)
            total = total + jnp.where(counts, states[off], 0.0)
        sums_ref[to * size : (to + 1) * size, :] = total
    total_ref[...] = (states[0] + states[1]) + (states[2] + states[3])


def grad_states(scale, place_ref, own, near, far, both, all_ref, sums_ref, total_ref):
    count = own.shape[0]
    width = own.shape[1] // 3
    states = []
    for off, ref in enumerate((own, near, far, both)):
        for k in range(3):
            column = slice(k * width, (k + 1) * width)
            x = ref[:count, column]
            if off:
                x = x * power(ref[count : count + 1, column])
            all_ref[off * count : (off + 1) * count, column] = x
        rows = all_ref[off * count : (off + 1) * count, :]
        states.append(scale * dot3(split(part(rows, 2, width).T), split(part(rows, 0, width))))
    group_sums(place_ref[0], states, sums_ref, total_ref, True)


def inner_key(scale, all_ref, out_ref):
    width = all_ref.shape[1] // 3
    count = all_ref.shape[0] // GROUP
    places = lax.broadcasted_iota(jnp.int32, (count, count), 0)
    others = lax.broadcasted_iota(jnp.int32, (count, count), 1)
    for off in range(GROUP):
        rows = all_ref[off * count : (off + 1) * count, :]
        scores = dot3(split(part(rows, 1, width)), split(part(rows, 2, width)), True)
        scores = jnp.where(others >= places, scores, 0.0)
        out_ref[off * count : (off + 1) * count, :] = scale * dot3(split(scores), split(part(rows, 0, width)))


def key_low(all_ref, sums_ref, before_ref, inner_ref, low_ref, grad_ref):
    width = all_ref.shape[1] // 3
    count = all_ref.shape[0] // GROUP
    for off in range(GROUP):
        grad = sums_ref[off * width : (off + 1) * width, :] + before_ref[...]
        grad_ref[off * width : (off + 1) * width, :] = grad
        span = slice(off * count, (off + 1) * count)
        carried = dot3(split(all_ref[span, width : 2 * width]), split(grad))
        low_ref[span, :] = (carried + inner_ref[span, :]).astype(BF16)


def pieces_of(tokens_ref, first_ref, first_other, last_ref, last_other, core):
    count, width = tokens_ref.shape
    half, side = count // 2, width // 2
    found = []
    for column in range(2):
        found.append((0, 0, count, column, tokens_ref, 0, column * side))
        for ref, whose in ((first_ref, core), (first_other, 1 - core)):
            for off in (1, 2):
                row = ((off - 1) * 2 + column) * half
                found.append((off, whose * half, half, column, ref, row, 0))
        for ref, whose in ((last_ref, core), (last_other, 1 - core)):
            found.append((3, whose * half, half, column, ref, column * half, 0))
    return found


def products(high, place_ref, tokens_ref, first_ref, first_other, last_ref, last_other, low_ref, sent_ref, kept_ref, turned, low_t):
    count, width = tokens_ref.shape
    side = width // 2
    core = place_ref[1]
    group = place_ref[2]
    sums = [None, None]
    for block, row, size, column, ref, at, left in pieces_of(tokens_ref, first_ref, first_other, last_ref, last_other, core):
        start = block * count + row
        if not isinstance(row, int):
            start = pl.multiple_of(start, size)
        low = low_ref[pl.ds(start, size), :].T
        term = jnp.dot(low, ref[at : at + size, left : left + side], preferred_element_type=F32)
        sums[column] = term if sums[column] is None else sums[column] + term
    turned[:, :side] = sums[0]
    turned[:, side:] = sums[1]
    groups = 1 << len(high)
    span = width // groups
    order = halving_order(high)
    for k, off in enumerate(order):
        start = pl.multiple_of((group ^ off // GROUP) * span, span)
        rows = turned[:, pl.ds(start, span)].T
        if k < groups // 2:
            kept_ref[k * span : (k + 1) * span, :] = rows
        else:
            k -= groups // 2
            sent_ref[k * span : (k + 1) * span, :] = rows.astype(BF16)


def halving_order(high):
    order = [0]
    for bit in high:
        order = [off + more for off in order for more in (0, bit)]
    return order


def key_states(layout, parts, place_ref, *refs):
    chunks = len(layout)
    (tokens_ref, first_ref, first_other, last_ref, last_other, all_ref,
     keys_ref, sums_ref, total_ref, weights, sem) = refs[chunks:]
    rows = weights.shape[0] // parts
    here, core = place_ref[3], place_ref[1]
    copies = []
    for ref, offsets in zip(refs[:chunks], layout, strict=True):
        for k, off in enumerate(offsets):
            start = pl.multiple_of((here ^ off) * rows, rows)
            copy = pltpu.make_async_copy(
                ref.at[pl.ds(k * rows, rows), :], weights.at[pl.ds(start, rows), :], sem.at[len(copies)]
            )
            copy.start()
            copies.append(copy)
    for copy in copies:
        copy.wait()
    count, width = tokens_ref.shape
    side = width // 2
    for block, row, size, column, ref, at, left in pieces_of(tokens_ref, first_ref, first_other, last_ref, last_other, core):
        start = block * count + row
        if not isinstance(row, int):
            start = pl.multiple_of(start, size)
        term = jnp.dot(
            ref[at : at + size, left : left + side],
            weights[column * side : (column + 1) * side, :],
            preferred_element_type=F32,
        )
        if column:
            term = keys_ref[pl.ds(start, size), :] + term
        keys_ref[pl.ds(start, size), :] = term
    head_dim = keys_ref.shape[1]
    states = []
    for off in range(GROUP):
        span = slice(off * count, (off + 1) * count)
        values = all_ref[span, head_dim : 2 * head_dim]
        states.append(dot3(split(values.T), split(keys_ref[span, :])))
    group_sums(place_ref[0], states, sums_ref, total_ref, False)


def inner_rest(scale, all_ref, keys_ref, grad_ref, value_ref, state_ref):
    width = keys_ref.shape[1]
    count = keys_ref.shape[0] // GROUP
    places = lax.broadcasted_iota(jnp.int32, (count, count), 0)
    others = lax.broadcasted_iota(jnp.int32, (count, count), 1)
    for off in range(GROUP):
        span = slice(off * count, (off + 1) * count)
        rows = all_ref[span, :]
        lifted, values, dout = (split(part(rows, k, width)) for k in range(3))
        keys = split(keys_ref[span, :])
        mixed = jnp.where(others >= places, dot3(keys, lifted, True), 0.0)
        carried = dot3(keys, split(grad_ref[off * width : (off + 1) * width, :]), True)
        value_ref[span, :] = carried + scale * dot3(split(mixed), dout)
        scores = jnp.where(places >= others, dot3(dout, values, True), 0.0)
        state_ref[span, :] = dot3(split(scores), keys)


def results(all_ref, sums_ref, before_ref, state_ref, value_ref, own, near, far, both):
    width = before_ref.shape[1]
    count = state_ref.shape[0] // GROUP
    for off, ref in enumerate((own, near, far, both)):
        span = slice(off * count, (off + 1) * count)
        before = sums_ref[off * width : (off + 1) * width, :] + before_ref[...]
        state = state_ref[span, :] + dot3(split(all_ref[span, 2 * width :]), split(before))
        ref[:, :width] = state.astype(ref.dtype)
        ref[:, width:] = value_ref[span, :].astype(ref.dtype)


def at_home(scale, place_ref, q_ref, routing_ref, gates_ref, own, near, far, both, query_ref, value_ref, gate_ref):
    queries, routing, gates = q_ref[...], routing_ref[...], gates_ref[...]
    width = queries.shape[1]
    query = jnp.zeros_like(queries)
    value = jnp.zeros_like(queries)
    gate = jnp.zeros(gate_ref.shape, F32)
    for off, ref in enumerate((own, near, far, both)):
        hit = routing == (place_ref[0] ^ off)
        weight = jnp.sum(jnp.where(hit, gates, 0.0), axis=1, keepdims=True)
        routed = jnp.sum(hit.astype(F32), axis=1, keepdims=True)
        state = ref[:, :width].astype(F32)
        query = query + weight * state
        value = value + routed * ref[:, width:].astype(F32)
        gate = gate + jnp.where(hit, jnp.sum(queries * state, axis=1, keepdims=True), 0.0)
    query_ref[...] = scale * query
    value_ref[...] = value
    gate_ref[...] = scale * gate


def by_column(place_ref, x_ref, own, near, far, both):
    size = own.shape[1]
    for off, ref in enumerate((own, near, far, both)):
        ref[...] = x_ref[:, pl.ds(pl.multiple_of((place_ref[0] ^ off) * size, size), size)]


def by_row(place_ref, x_ref, got_ref, own, near, far, both, room):
    size = own.shape[0]
    room[...] = x_ref[...] + got_ref[...].astype(F32)
    for off, ref in enumerate((own, near, far, both)):
        ref[...] = room[pl.ds(pl.multiple_of((place_ref[0] ^ off) * size, size), size), :]


def in_columns(place_ref, own, near, far, both, out_ref):
    size = own.shape[1]
    for off, ref in enumerate((own, near, far, both)):
        out_ref[:, pl.ds(pl.multiple_of((place_ref[0] ^ off) * size, size), size)] = ref[...]


def swap(x, off, parts):
    return lax.ppermute(x, "ctx", [(i, i ^ off) for i in range(parts)])


def one_way(x, off, parts, reverse):
    sources = [i for i in range(parts) if bool(i & off) == reverse]
    return lax.ppermute(x, "ctx", [(i, i ^ off) for i in sources])


def other_core(x):
    return lax.ppermute(x, "head", [(i, i ^ 1) for i in range(lax.axis_size("head"))])


def prefix(total, bits, parts, here, reverse):
    before = jnp.zeros_like(total)
    for bit in bits[:-1]:
        got = swap(total, bit, parts)
        before = before + jnp.where(((here & bit) == 0) == reverse, got, 0.0)
        total = total + got
    return before + one_way(total, bits[-1], parts, reverse)


def on_device(tokens, queries, values, dout, key_weight, routing, gates):
    count, width = tokens.shape
    rows, memories, head_dim = key_weight.shape
    parts = lax.axis_size("ctx")
    high = [1 << k for k in range(2, parts.bit_length() - 1)]
    here = lax.axis_index("ctx").astype(jnp.int32)
    core = lax.axis_index("head").astype(jnp.int32) & 1
    at = jnp.stack([here & (GROUP - 1), core, here // GROUP, here])
    scale = 1.0 / math.sqrt(head_dim * count * parts)
    tall = GROUP * count
    smem = pl.BlockSpec(memory_space=pltpu.SMEM)
    vmem = pl.BlockSpec(memory_space=pltpu.VMEM)
    anywhere = pl.BlockSpec(memory_space=pl.ANY)

    def shape(r, c, dtype=F32):
        return jax.ShapeDtypeStruct((r, c), dtype)

    mine = call(
        by_column,
        [shape(rows, head_dim, BF16)] * 4,
        at, key_weight.reshape(rows, memories * head_dim),
        spaces=[smem, vmem],
    )
    weights = [mine[0]] + [swap(mine[off], off, parts) for off in (1, 2, 3)]

    half = lax.dynamic_slice(tokens, (core * (count // 2), jnp.int32(0)), (count // 2, width))
    left, right = half[:, : width // 2], half[:, width // 2 :]
    left_x, right_y = swap(left, 1, parts), swap(right, 2, parts)

    sent = call(
        messages,
        [shape(count, 3 * head_dim)] + [shape(count + TAIL, 3 * head_dim)] * 3,
        at, queries, values, dout, routing, gates,
        spaces=[smem] + [vmem] * 5,
    )
    got = [swap(sent[off].astype(F16), off, parts).astype(F32) for off in (1, 2, 3)]

    right_x, left_y = swap(right, 1, parts), swap(left, 2, parts)
    first = jnp.concatenate([left_x, right_x, left_y, right_y], axis=0)
    last = jnp.concatenate([swap(left_x, 2, parts), swap(right_y, 1, parts)], axis=0)

    block = jnp.concatenate(weights, axis=0)
    held = [0, 1, 2, 3]
    for bit in reversed(high):
        block = jnp.concatenate([block, swap(block, bit, parts)], axis=0)
        held = held + [off ^ bit for off in held]

    every, grad_sums, total = call(
        functools.partial(grad_states, scale),
        [shape(tall, 3 * head_dim), shape(GROUP * head_dim, head_dim), shape(head_dim, head_dim)],
        at, sent[0], *got,
        spaces=[smem] + [vmem] * 4,
        flops=6 * tall * head_dim * head_dim,
    )
    before = prefix(total, high, parts, here, True)
    inner_k = call(
        functools.partial(inner_key, scale),
        shape(tall, head_dim),
        every,
        flops=12 * tall * count * head_dim,
    )
    low, grad_in = call(
        key_low,
        [shape(tall, head_dim, BF16), shape(GROUP * head_dim, head_dim)],
        every, grad_sums, before, inner_k,
        flops=6 * tall * head_dim * head_dim,
    )

    first_other, last_other = other_core(first), other_core(last)
    group_tokens = (tokens, first, first_other, last, last_other)

    sent, kept = call(
        functools.partial(products, high),
        [shape(width // 2, head_dim, BF16), shape(width // 2, head_dim)],
        at, *group_tokens, low,
        spaces=[smem] + [vmem] * 6,
        scratch=[pltpu.VMEM((head_dim, width), F32), pltpu.VMEM((head_dim, tall), BF16)],
        flops=2 * tall * width * head_dim,
    )
    reduced = swap(sent, high[0], parts)
    for bit in high[1:]:
        size = kept.shape[0] // 2
        sent = (kept[size:] + reduced[size:].astype(F32)).astype(BF16)
        kept = kept[:size] + reduced[:size].astype(F32)
        reduced = swap(sent, bit, parts)
    mine = call(
        by_row,
        [shape(rows, head_dim)] * 4,
        at, kept, reduced,
        spaces=[smem, vmem, vmem],
        scratch=[pltpu.VMEM((GROUP * rows, head_dim), F32)],
    )
    key_grad = call(
        in_columns,
        shape(rows, memories * head_dim),
        at, mine[0], *[swap(mine[off], off, parts) for off in (1, 2, 3)],
        spaces=[smem] + [vmem] * 4,
    ).reshape(rows, memories, head_dim)

    keys, sums, total = call(
        functools.partial(key_states, [held], parts),
        [shape(tall, head_dim), shape(GROUP * head_dim, head_dim), shape(head_dim, head_dim)],
        at, block, *group_tokens, every,
        spaces=[smem, anywhere] + [vmem] * 6,
        scratch=[pltpu.VMEM((width, head_dim), BF16), pltpu.SemaphoreType.DMA((parts,))],
        flops=2 * tall * width * head_dim,
    )
    before = prefix(total, high, parts, here, False)
    inner_v, inner_state = call(
        functools.partial(inner_rest, scale),
        [shape(tall, head_dim)] * 2,
        every, keys, grad_in,
        flops=24 * tall * count * head_dim,
    )
    sent = call(
        results,
        [shape(count, 2 * head_dim)] + [shape(count, 2 * head_dim, BF16)] * 3,
        every, sums, before, inner_state, inner_v,
        flops=6 * tall * head_dim * head_dim,
    )
    query_grad, value_grad, gate_part = call(
        functools.partial(at_home, scale),
        [shape(count, head_dim), shape(count, head_dim), shape(count, routing.shape[1])],
        at, queries, routing, gates, sent[0], *[swap(sent[off], off, parts) for off in (1, 2, 3)],
        spaces=[smem] + [vmem] * 7,
    )
    gate_grad = lax.psum(gate_part, "head")
    return (key_grad, query_grad, value_grad, gate_grad)


def solution(mesh):
    return jax.shard_map(
        on_device,
        mesh=mesh,
        in_specs=(
            P("ctx", None),
            P("ctx", "head"),
            P("ctx", "head"),
            P("ctx", "head"),
            P("ctx", None, "head"),
            P("ctx", None),
            P("ctx", None),
        ),
        out_specs=(P("ctx", None, "head"), P("ctx", "head"), P("ctx", "head"), P("ctx", None)),
        check_vma=False,
    )
```

```python
import functools
import math

import jax
import jax.numpy as jnp
from jax import lax
from jax.experimental import pallas as pl
from jax.experimental.pallas import tpu as pltpu
from jax.sharding import PartitionSpec as P

F32 = jnp.float32
BF16 = jnp.bfloat16
F16 = jnp.float16
GROUP = 4
TAIL = 16


def split(x):
    high = x.astype(BF16)
    return high, (x - high.astype(F32)).astype(BF16)


def dot3(a, b, b_last=False):
    dims = (((1,), (1 if b_last else 0,)), ((), ()))

    def one(x, y):
        return lax.dot_general(x, y, dims, preferred_element_type=F32)

    return one(a[0], b[0]) + (one(a[0], b[1]) + one(a[1], b[0]))


def part(x, k, width):
    return x[:, k * width : (k + 1) * width]


def call(body, outs, *args, scratch=(), spaces=None, flops=0, room=20):
    vmem = pl.BlockSpec(memory_space=pltpu.VMEM)
    size = sum(a.size * a.dtype.itemsize for a in args)
    return pl.pallas_call(
        body,
        out_shape=outs,
        in_specs=[vmem] * len(args) if spaces is None else spaces,
        out_specs=jax.tree.map(lambda _: vmem, outs),
        scratch_shapes=list(scratch),
        cost_estimate=pl.CostEstimate(flops=flops, bytes_accessed=size, transcendentals=0),
        compiler_params=pltpu.CompilerParams(vmem_limit_bytes=room * 1024 * 1024),
    )(*args)


def exponent(x):
    top = jnp.max(jnp.abs(x), axis=(0, 1), keepdims=True)
    return jnp.clip(jnp.ceil(jnp.log(jnp.maximum(top, 1e-30)) * (1.0 / math.log(2.0))), -90.0, 40.0) - 14.0


def power(k):
    return jnp.exp(k * math.log(2.0))


def fetch(refs, rooms, sem):
    copies = [pltpu.make_async_copy(ref, room, sem.at[k]) for k, (ref, room) in enumerate(zip(refs, rooms, strict=True))]
    for copy in copies:
        copy.start()
    for copy in copies:
        copy.wait()


def messages(place_ref, q_at, v_at, dout_at, routing_at, gates_at, own, near, far, both, q_ref, v_ref, dout_ref, routing_ref, gates_ref, sem):
    fetch((q_at, v_at, dout_at, routing_at, gates_at), (q_ref, v_ref, dout_ref, routing_ref, gates_ref), sem)
    count, width = q_ref.shape
    routing, gates = routing_ref[...].T, gates_ref[...].T
    place = place_ref[0]
    q, v, dout = q_ref[...], v_ref[...], dout_ref[...]
    exponents = [exponent(x) for x in (q, v, dout)]
    scales = [1.0 / power(k) for k in exponents]
    for off, ref in enumerate((own, near, far, both)):
        hit = routing == (place ^ off)
        weight = jnp.sum(jnp.where(hit, gates, 0.0), axis=1, keepdims=True)
        routed = jnp.sum(hit.astype(F32), axis=1, keepdims=True)
        for k, x in enumerate((weight * q, routed * v, dout)):
            column = slice(k * width, (k + 1) * width)
            if off:
                ref[:count, column] = x * scales[k]
                ref[count:, column] = jnp.broadcast_to(exponents[k], (TAIL, width))
            else:
                ref[:, column] = x


def group_sums(place, states, sums_ref, total_ref, reverse):
    size = states[0].shape[0]
    for to in range(GROUP):
        total = jnp.zeros_like(states[0])
        for off in range(GROUP):
            counts = (place ^ off) > (place ^ to) if reverse else (place ^ off) < (place ^ to)
            total = total + jnp.where(counts, states[off], 0.0)
        sums_ref[to * size : (to + 1) * size, :] = total
    total_ref[...] = (states[0] + states[1]) + (states[2] + states[3])


def grad_states(scale, place_ref, own, near, far, both, all_ref, sums_ref, total_ref):
    count = own.shape[0]
    width = own.shape[1] // 3
    states = []
    for off, ref in enumerate((own, near, far, both)):
        for k in range(3):
            column = slice(k * width, (k + 1) * width)
            x = ref[:count, column]
            if off:
                x = x * power(ref[count : count + 1, column])
            all_ref[off * count : (off + 1) * count, column] = x
        rows = all_ref[off * count : (off + 1) * count, :]
        states.append(scale * dot3(split(part(rows, 2, width).T), split(part(rows, 0, width))))
    group_sums(place_ref[0], states, sums_ref, total_ref, True)


def inner_key(scale, all_ref, out_ref):
    width = all_ref.shape[1] // 3
    count = all_ref.shape[0] // GROUP
    places = lax.broadcasted_iota(jnp.int32, (count, count), 0)
    others = lax.broadcasted_iota(jnp.int32, (count, count), 1)
    for off in range(GROUP):
        rows = all_ref[off * count : (off + 1) * count, :]
        scores = dot3(split(part(rows, 1, width)), split(part(rows, 2, width)), True)
        scores = jnp.where(others >= places, scores, 0.0)
        out_ref[off * count : (off + 1) * count, :] = scale * dot3(split(scores), split(part(rows, 0, width)))


def key_low(all_ref, sums_ref, before_ref, inner_ref, low_ref, grad_ref):
    width = all_ref.shape[1] // 3
    count = all_ref.shape[0] // GROUP
    for off in range(GROUP):
        grad = sums_ref[off * width : (off + 1) * width, :] + before_ref[...]
        grad_ref[off * width : (off + 1) * width, :] = grad
        span = slice(off * count, (off + 1) * count)
        carried = dot3(split(all_ref[span, width : 2 * width]), split(grad))
        low_ref[span, :] = (carried + inner_ref[span, :]).astype(BF16)


def pack(*refs):
    sources, out_ref, sem = refs[:-2], refs[-2], refs[-1]
    copies, at = [], 0
    for k, ref in enumerate(sources):
        copies.append(pltpu.make_async_copy(ref, out_ref.at[pl.ds(at, ref.shape[0]), :], sem.at[k]))
        at += ref.shape[0]
    for copy in copies:
        copy.start()
    for copy in copies:
        copy.wait()


def row_order(core, count):
    half = count // 2
    found = [(0, 0, count)]
    for whose in (core, 1 - core):
        for block in (1, 2):
            found.append((block, whose * half, half))
    for whose in (core, 1 - core):
        found.append((3, whose * half, half))
    return [
        (pl.multiple_of(block * count + row, size), size) if block else (0, size) for block, row, size in found
    ]


def first_products(place_ref, own, mine, other, low_ref, out_ref, last_low_ref, room):
    at = 0
    for start, size in row_order(place_ref[1], own.shape[0]):
        room[at : at + size, :] = low_ref[pl.ds(start, size), :]
        at += size
    low = room[...].T
    at, total = 0, None
    for ref in (own, mine, other):
        term = jnp.dot(low[:, at : at + ref.shape[0]], ref[...], preferred_element_type=F32)
        total = term if total is None else total + term
        at += ref.shape[0]
    out_ref[...] = total
    last_low_ref[...] = low[:, at:]


def products(steps, place_ref, first_ref, low_ref, last, last_other, *refs):
    outs, turned = refs[:-1], refs[-1]
    half, width = last.shape
    turned[...] = first_ref[...] + (
        jnp.dot(low_ref[:, :half], last[...], preferred_element_type=F32)
        + jnp.dot(low_ref[:, half:], last_other[...], preferred_element_type=F32)
    )
    group = place_ref[2]
    span = width // len(steps)
    for off, ref in zip(steps, outs, strict=True):
        start = pl.multiple_of((group ^ off // GROUP) * span, span)
        ref[...] = turned[:, pl.ds(start, span)].T.astype(ref.dtype)


def first_keys(layout, parts, place_ref, *refs):
    chunks = len(layout)
    own, mine, other, keys_ref, weights = refs[chunks:]
    rows = weights.shape[0] // parts
    here = place_ref[3]
    for ref, offsets in zip(refs[:chunks], layout, strict=True):
        for k, off in enumerate(offsets):
            start = pl.multiple_of((here ^ off) * rows, rows)
            weights[pl.ds(start, rows), :] = ref[k * rows : (k + 1) * rows, :]
    at = 0
    for ref in (own, mine, other):
        keys_ref[at : at + ref.shape[0], :] = jnp.dot(ref[...], weights[...], preferred_element_type=F32)
        at += ref.shape[0]


def key_states(place_ref, first_ref, weights, last, last_other, all_ref, keys_ref, sums_ref, total_ref):
    count = all_ref.shape[0] // GROUP
    half, head_dim = last.shape[0], keys_ref.shape[1]
    at = 0
    order = row_order(place_ref[1], count)
    for start, size in order[:-2]:
        keys_ref[pl.ds(start, size), :] = first_ref[at : at + size, :]
        at += size
    for (start, size), ref in zip(order[-2:], (last, last_other), strict=True):
        keys_ref[pl.ds(start, size), :] = jnp.dot(ref[...], weights[...], preferred_element_type=F32)
    states = []
    for off in range(GROUP):
        span = slice(off * count, (off + 1) * count)
        values = all_ref[span, head_dim : 2 * head_dim]
        states.append(dot3(split(values.T), split(keys_ref[span, :])))
    group_sums(place_ref[0], states, sums_ref, total_ref, False)


def inner_rest(scale, all_ref, keys_ref, grad_ref, value_ref, state_ref):
    width = keys_ref.shape[1]
    count = keys_ref.shape[0] // GROUP
    places = lax.broadcasted_iota(jnp.int32, (count, count), 0)
    others = lax.broadcasted_iota(jnp.int32, (count, count), 1)
    for off in range(GROUP):
        span = slice(off * count, (off + 1) * count)
        rows = all_ref[span, :]
        lifted, values, dout = (split(part(rows, k, width)) for k in range(3))
        keys = split(keys_ref[span, :])
        mixed = jnp.where(others >= places, dot3(keys, lifted, True), 0.0)
        carried = dot3(keys, split(grad_ref[off * width : (off + 1) * width, :]), True)
        value_ref[span, :] = carried + scale * dot3(split(mixed), dout)
        scores = jnp.where(places >= others, dot3(dout, values, True), 0.0)
        state_ref[span, :] = dot3(split(scores), keys)


def results(all_ref, sums_ref, before_ref, state_ref, value_ref, own, near, far, both):
    width = before_ref.shape[1]
    count = state_ref.shape[0] // GROUP
    for off, ref in enumerate((own, near, far, both)):
        span = slice(off * count, (off + 1) * count)
        before = sums_ref[off * width : (off + 1) * width, :] + before_ref[...]
        state = state_ref[span, :] + dot3(split(all_ref[span, 2 * width :]), split(before))
        ref[:, :width] = state.astype(ref.dtype)
        ref[:, width:] = value_ref[span, :].astype(ref.dtype)


def at_home(scale, place_ref, q_ref, routing_ref, gates_ref, own, near, far, both, query_ref, value_ref, gate_ref):
    queries, routing, gates = q_ref[...], routing_ref[...].T, gates_ref[...].T
    width = queries.shape[1]
    query = jnp.zeros_like(queries)
    value = jnp.zeros_like(queries)
    gate = jnp.zeros(gate_ref.shape[::-1], F32)
    for off, ref in enumerate((own, near, far, both)):
        hit = routing == (place_ref[0] ^ off)
        weight = jnp.sum(jnp.where(hit, gates, 0.0), axis=1, keepdims=True)
        routed = jnp.sum(hit.astype(F32), axis=1, keepdims=True)
        state = ref[:, :width].astype(F32)
        query = query + weight * state
        value = value + routed * ref[:, width:].astype(F32)
        gate = gate + jnp.where(hit, jnp.sum(queries * state, axis=1, keepdims=True), 0.0)
    query_ref[...] = scale * query
    value_ref[...] = value
    gate_ref[...] = (scale * gate).T


def by_column(place_ref, x_ref, own, near, far, both):
    size = own.shape[1]
    for off, ref in enumerate((own, near, far, both)):
        ref[...] = x_ref[:, pl.ds(pl.multiple_of((place_ref[0] ^ off) * size, size), size)]


def by_row(place_ref, *refs):
    parts, (own, near, far, both, room) = refs[:-5], refs[-5:]
    size = own.shape[0]
    total = parts[0][...]
    for ref in parts[1:]:
        total = total + ref[...].astype(F32)
    room[...] = total
    for off, ref in enumerate((own, near, far, both)):
        ref[...] = room[pl.ds(pl.multiple_of((place_ref[0] ^ off) * size, size), size), :]


def in_columns(place_ref, own, near, far, both, out_ref):
    size = own.shape[1]
    for off, ref in enumerate((own, near, far, both)):
        out_ref[:, pl.ds(pl.multiple_of((place_ref[0] ^ off) * size, size), size)] = ref[...]


def after(x, *others):
    return lax.optimization_barrier((x, *others))[0]


def swap(x, off, parts):
    return lax.ppermute(x, "ctx", [(i, i ^ off) for i in range(parts)])


def other_core(x):
    return lax.ppermute(x, "head", [(i, i ^ 1) for i in range(lax.axis_size("head"))])


def from_groups(total, steps, parts):
    return [swap(total, off, parts) for off in steps[1:]]


def prefix(total, got, steps, here, reverse):
    before = jnp.zeros_like(total)
    for off, x in zip(steps[1:], got, strict=True):
        other = here ^ off
        before = before + jnp.where(other > here if reverse else other < here, x, 0.0)
    return before


def over_heads(x):
    count = lax.axis_size("head")
    bit = 1
    while bit < count:
        x = x + lax.ppermute(x, "head", [(i, i ^ bit) for i in range(count)])
        bit *= 2
    return x


def on_device(tokens, queries, values, dout, key_weight, routing, gates):
    count, width = tokens.shape
    rows, memories, head_dim = key_weight.shape
    parts = lax.axis_size("ctx")
    steps = list(range(0, parts, GROUP))
    here = lax.axis_index("ctx").astype(jnp.int32)
    core = lax.axis_index("head").astype(jnp.int32) & 1
    at = jnp.stack([here & (GROUP - 1), core, here // GROUP, here])
    scale = 1.0 / math.sqrt(head_dim * count * parts)
    tall = GROUP * count
    smem = pl.BlockSpec(memory_space=pltpu.SMEM)
    vmem = pl.BlockSpec(memory_space=pltpu.VMEM)
    anywhere = pl.BlockSpec(memory_space=pl.ANY)

    def shape(r, c, dtype=F32):
        return jax.ShapeDtypeStruct((r, c), dtype)

    def stack(*blocks):
        size = sum(x.shape[0] for x in blocks)
        return call(
            pack,
            shape(size, blocks[0].shape[1], blocks[0].dtype),
            *blocks,
            spaces=[anywhere] * len(blocks),
            scratch=[pltpu.SemaphoreType.DMA((len(blocks),))],
        )

    half = lax.dynamic_slice(tokens, (core * (count // 2), jnp.int32(0)), (count // 2, width))
    from_x, from_y = swap(half, 1, parts), swap(half, 2, parts)

    mine = call(
        by_column,
        [shape(rows, head_dim, BF16)] * 4,
        at, key_weight.reshape(rows, memories * head_dim),
        spaces=[smem, vmem],
    )
    weights = [mine[0]] + [swap(mine[off], off, parts) for off in (1, 2, 3)]

    sent = call(
        messages,
        [shape(count, 3 * head_dim)] + [shape(count + TAIL, 3 * head_dim)] * 3,
        at, queries, values, dout, routing.T, gates.T,
        spaces=[smem] + [anywhere] * 5,
        scratch=[pltpu.VMEM((count, head_dim), F32)] * 3
        + [pltpu.VMEM(x.shape[::-1], x.dtype) for x in (routing, gates)]
        + [pltpu.SemaphoreType.DMA((5,))],
    )
    coded = [x.astype(F16) for x in sent[1:]]
    got = [swap(x, off, parts).astype(F32) for off, x in zip((1, 2, 3), coded)]

    neighbours = stack(after(from_x, *coded, *weights), from_y)
    neighbours_other = other_core(neighbours)

    block = stack(after(weights[0], *coded), *weights[1:])
    chunks, layout, held = [block], [list(range(GROUP))], list(range(GROUP))
    bit = parts // 2
    while bit >= GROUP:
        other = swap(block, bit, parts)
        chunks.append(other)
        layout.append([off ^ bit for off in held])
        held = held + layout[-1]
        if bit > GROUP:
            block = stack(block, after(other, neighbours_other))
        bit //= 2

    last_a = swap(after(from_x, neighbours_other, *got)[: count // 4], 2, parts)
    last_b = swap(after(from_y, neighbours_other, *got)[count // 4 :], 1, parts)

    every, grad_sums, total = call(
        functools.partial(grad_states, scale),
        [shape(tall, 3 * head_dim), shape(GROUP * head_dim, head_dim), shape(head_dim, head_dim)],
        at, after(sent[0], neighbours_other), *got,
        spaces=[smem] + [vmem] * 4,
        flops=6 * tall * head_dim * head_dim,
    )
    totals = from_groups(total, steps, parts)
    before = prefix(total, totals, steps, here, True)
    inner_k = call(
        functools.partial(inner_key, scale),
        shape(tall, head_dim),
        every,
        flops=12 * tall * count * head_dim,
    )
    low, grad_in = call(
        key_low,
        [shape(tall, head_dim, BF16), shape(GROUP * head_dim, head_dim)],
        every, grad_sums, before, inner_k,
        flops=6 * tall * head_dim * head_dim,
    )

    first, weights = call(
        functools.partial(first_keys, layout, parts),
        [shape(3 * count, head_dim), shape(width, head_dim, BF16)],
        at, *chunks, tokens, neighbours, neighbours_other,
        spaces=[smem] + [vmem] * (3 + len(chunks)),
        flops=2 * tall * width * head_dim,
    )
    product, last_low = call(
        first_products,
        [shape(head_dim, width), shape(head_dim, count, BF16)],
        at, tokens, neighbours, neighbours_other, low,
        spaces=[smem] + [vmem] * 4,
        scratch=[pltpu.VMEM((tall, head_dim), BF16)],
        flops=2 * tall * width * head_dim,
    )
    last = stack(after(last_a, first, *totals), last_b)
    last_other = other_core(last)

    keys, sums, key_total = call(
        key_states,
        [shape(tall, head_dim), shape(GROUP * head_dim, head_dim), shape(head_dim, head_dim)],
        at, first, weights, last, last_other, every,
        spaces=[smem] + [vmem] * 5,
        flops=2 * count * width * head_dim,
    )
    key_totals = from_groups(key_total, steps, parts)

    span = width // len(steps)
    sent = call(
        functools.partial(products, steps),
        [shape(span, head_dim)] + [shape(span, head_dim, BF16)] * (len(steps) - 1),
        at, product, after(last_low, key_total), last, last_other,
        spaces=[smem] + [vmem] * 4,
        scratch=[pltpu.VMEM((head_dim, width), F32)],
        flops=2 * count * width * head_dim,
    )
    parts_of_sum = [sent[0]] + [swap(x, off, parts) for off, x in zip(steps[1:], sent[1:], strict=True)]
    inner_v, inner_state = call(
        functools.partial(inner_rest, scale),
        [shape(tall, head_dim)] * 2,
        every, after(keys, sent[0]), grad_in,
        flops=24 * tall * count * head_dim,
    )

    mine = call(
        by_row,
        [shape(rows, head_dim)] * 4,
        at, *parts_of_sum,
        spaces=[smem] + [vmem] * len(steps),
        scratch=[pltpu.VMEM((GROUP * rows, head_dim), F32)],
    )
    others = [swap(mine[off], off, parts) for off in (1, 2, 3)]

    before = prefix(key_total, key_totals, steps, here, False)
    sent = call(
        results,
        [shape(count, 2 * head_dim)] + [shape(count, 2 * head_dim, BF16)] * 3,
        every, sums, before, inner_state, inner_v,
        flops=6 * tall * head_dim * head_dim,
    )
    query_grad, value_grad, gate_part = call(
        functools.partial(at_home, scale),
        [shape(count, head_dim), shape(count, head_dim), shape(routing.shape[1], count)],
        at, queries, routing.T, gates.T, sent[0], *[swap(sent[off], off, parts) for off in (1, 2, 3)],
        spaces=[smem] + [vmem] * 7,
    )
    gate_grad = over_heads(after(gate_part, *mine)).T
    key_grad = call(
        in_columns,
        shape(rows, memories * head_dim),
        at, mine[0], *others,
        spaces=[smem] + [vmem] * 4,
    ).reshape(rows, memories, head_dim)
    return (key_grad, query_grad, value_grad, gate_grad)


def solution(mesh):
    return jax.shard_map(
        on_device,
        mesh=mesh,
        in_specs=(
            P("ctx", None),
            P("ctx", "head"),
            P("ctx", "head"),
            P("ctx", "head"),
            P("ctx", None, "head"),
            P("ctx", None),
            P("ctx", None),
        ),
        out_specs=(P("ctx", None, "head"), P("ctx", "head"), P("ctx", "head"), P("ctx", None)),
        check_vma=False,
    )
```

```python
import functools
import math

import jax
import jax.numpy as jnp
from jax import lax
from jax.experimental import pallas as pl
from jax.experimental.pallas import tpu as pltpu
from jax.sharding import PartitionSpec as P

F32 = jnp.float32
BF16 = jnp.bfloat16
F16 = jnp.float16
GROUP = 4
TAIL = 16


def split(x):
    high = x.astype(BF16)
    return high, (x - high.astype(F32)).astype(BF16)


def dot3(a, b, b_last=False):
    dims = (((1,), (1 if b_last else 0,)), ((), ()))

    def one(x, y):
        return lax.dot_general(x, y, dims, preferred_element_type=F32)

    return one(a[0], b[0]) + (one(a[0], b[1]) + one(a[1], b[0]))


def part(x, k, width):
    return x[:, k * width : (k + 1) * width]


def call(body, outs, *args, scratch=(), spaces=None, flops=0, waits=()):
    vmem = pl.BlockSpec(memory_space=pltpu.VMEM)
    size = sum(a.size * a.dtype.itemsize for a in args)
    count = len(args)

    def kernel(*refs):
        body(*refs[:count], *refs[count + len(waits) :])

    return pl.pallas_call(
        kernel,
        out_shape=outs,
        in_specs=([vmem] * count if spaces is None else spaces) + [pl.BlockSpec(memory_space=pl.ANY)] * len(waits),
        out_specs=jax.tree.map(lambda _: vmem, outs),
        scratch_shapes=list(scratch),
        cost_estimate=pl.CostEstimate(flops=flops, bytes_accessed=size, transcendentals=0),
        compiler_params=pltpu.CompilerParams(vmem_limit_bytes=20 * 1024 * 1024),
    )(*args, *waits)


def exponent(x):
    top = jnp.max(jnp.abs(x), axis=(0, 1), keepdims=True)
    return jnp.clip(jnp.ceil(jnp.log(jnp.maximum(top, 1e-30)) * (1.0 / math.log(2.0))), -90.0, 40.0) - 14.0


def power(k):
    return jnp.exp(k * math.log(2.0))


def fetch(refs, rooms, sem):
    copies = [pltpu.make_async_copy(ref, room, sem.at[k]) for k, (ref, room) in enumerate(zip(refs, rooms, strict=True))]
    for copy in copies:
        copy.start()
    for copy in copies:
        copy.wait()


def messages(place_ref, q_at, v_at, dout_at, routing_at, gates_at, own, near, far, both, q_ref, v_ref, dout_ref, routing_ref, gates_ref, sem):
    fetch((q_at, v_at, dout_at, routing_at, gates_at), (q_ref, v_ref, dout_ref, routing_ref, gates_ref), sem)
    count, width = q_ref.shape
    routing, gates = routing_ref[...].T, gates_ref[...].T
    place = place_ref[0]
    q, v, dout = q_ref[...], v_ref[...], dout_ref[...]
    exponents = [exponent(x) for x in (q, v, dout)]
    scales = [1.0 / power(k) for k in exponents]
    for off, ref in enumerate((own, near, far, both)):
        hit = routing == (place ^ off)
        weight = jnp.sum(jnp.where(hit, gates, 0.0), axis=1, keepdims=True)
        routed = jnp.sum(hit.astype(F32), axis=1, keepdims=True)
        for k, x in enumerate((weight * q, routed * v, dout)):
            column = slice(k * width, (k + 1) * width)
            if off:
                ref[:count, column] = x * scales[k]
                ref[count:, column] = jnp.broadcast_to(exponents[k], (TAIL, width))
            else:
                ref[:, column] = x


def group_sums(place, states, sums_ref, total_ref, reverse):
    size = states[0].shape[0]
    for to in range(GROUP):
        total = jnp.zeros_like(states[0])
        for off in range(GROUP):
            counts = (place ^ off) > (place ^ to) if reverse else (place ^ off) < (place ^ to)
            total = total + jnp.where(counts, states[off], 0.0)
        sums_ref[to * size : (to + 1) * size, :] = total
    total_ref[...] = (states[0] + states[1]) + (states[2] + states[3])


def grad_states(scale, place_ref, own, near, far, both, all_ref, sums_ref, total_ref):
    count = own.shape[0]
    width = own.shape[1] // 3
    states = []
    for off, ref in enumerate((own, near, far, both)):
        for k in range(3):
            column = slice(k * width, (k + 1) * width)
            x = ref[:count, column]
            if off:
                x = x * power(ref[count : count + 1, column])
            all_ref[off * count : (off + 1) * count, column] = x
        rows = all_ref[off * count : (off + 1) * count, :]
        states.append(scale * dot3(split(part(rows, 2, width).T), split(part(rows, 0, width))))
    group_sums(place_ref[0], states, sums_ref, total_ref, True)


def inner_key(scale, all_ref, out_ref):
    width = all_ref.shape[1] // 3
    count = all_ref.shape[0] // GROUP
    places = lax.broadcasted_iota(jnp.int32, (count, count), 0)
    others = lax.broadcasted_iota(jnp.int32, (count, count), 1)
    for off in range(GROUP):
        rows = all_ref[off * count : (off + 1) * count, :]
        scores = dot3(split(part(rows, 1, width)), split(part(rows, 2, width)), True)
        scores = jnp.where(others >= places, scores, 0.0)
        out_ref[off * count : (off + 1) * count, :] = scale * dot3(split(scores), split(part(rows, 0, width)))


def key_low(all_ref, sums_ref, before_ref, inner_ref, low_ref, grad_ref):
    width = all_ref.shape[1] // 3
    count = all_ref.shape[0] // GROUP
    for off in range(GROUP):
        grad = sums_ref[off * width : (off + 1) * width, :] + before_ref[...]
        grad_ref[off * width : (off + 1) * width, :] = grad
        span = slice(off * count, (off + 1) * count)
        carried = dot3(split(all_ref[span, width : 2 * width]), split(grad))
        low_ref[span, :] = (carried + inner_ref[span, :]).astype(BF16)


def pack(*refs):
    sources, out_ref, sem = refs[:-2], refs[-2], refs[-1]
    copies, at = [], 0
    for k, ref in enumerate(sources):
        copies.append(pltpu.make_async_copy(ref, out_ref.at[pl.ds(at, ref.shape[0]), :], sem.at[k]))
        at += ref.shape[0]
    for copy in copies:
        copy.start()
    for copy in copies:
        copy.wait()


def cut(x_ref, y_ref, a_ref, b_ref, sem):
    size = a_ref.shape[0]
    copies = [
        pltpu.make_async_copy(x_ref.at[pl.ds(0, size), :], a_ref, sem.at[0]),
        pltpu.make_async_copy(y_ref.at[pl.ds(size, size), :], b_ref, sem.at[1]),
    ]
    for copy in copies:
        copy.start()
    for copy in copies:
        copy.wait()


def row_order(core, count):
    half = count // 2
    found = [(0, 0, count)]
    for whose in (core, 1 - core):
        for block in (1, 2):
            found.append((block, whose * half, half))
    for whose in (core, 1 - core):
        found.append((3, whose * half, half))
    return [
        (pl.multiple_of(block * count + row, size), size) if block else (0, size) for block, row, size in found
    ]


def first_products(place_ref, own, mine, other, low_ref, out_ref, last_low_ref, room):
    at = 0
    for start, size in row_order(place_ref[1], own.shape[0]):
        room[at : at + size, :] = low_ref[pl.ds(start, size), :]
        at += size
    low = room[...].T
    at, total = 0, None
    for ref in (own, mine, other):
        term = jnp.dot(low[:, at : at + ref.shape[0]], ref[...], preferred_element_type=F32)
        total = term if total is None else total + term
        at += ref.shape[0]
    out_ref[...] = total
    last_low_ref[...] = low[:, at:]


def products(steps, place_ref, first_ref, low_ref, last, last_other, *refs):
    outs, turned = refs[:-1], refs[-1]
    half, width = last.shape
    turned[...] = first_ref[...] + (
        jnp.dot(low_ref[:, :half], last[...], preferred_element_type=F32)
        + jnp.dot(low_ref[:, half:], last_other[...], preferred_element_type=F32)
    )
    group = place_ref[2]
    span = width // len(steps)
    for off, ref in zip(steps, outs, strict=True):
        start = pl.multiple_of((group ^ off // GROUP) * span, span)
        ref[...] = turned[:, pl.ds(start, span)].T.astype(ref.dtype)


def first_keys(layout, parts, place_ref, *refs):
    chunks = len(layout)
    own, mine, other, keys_ref, weights = refs[chunks:]
    rows = weights.shape[0] // parts
    here = place_ref[3]
    for ref, offsets in zip(refs[:chunks], layout, strict=True):
        for k, off in enumerate(offsets):
            start = pl.multiple_of((here ^ off) * rows, rows)
            weights[pl.ds(start, rows), :] = ref[k * rows : (k + 1) * rows, :]
    at = 0
    for ref in (own, mine, other):
        keys_ref[at : at + ref.shape[0], :] = jnp.dot(ref[...], weights[...], preferred_element_type=F32)
        at += ref.shape[0]


def key_states(place_ref, first_ref, weights, last, last_other, all_ref, keys_ref, sums_ref, total_ref):
    count = all_ref.shape[0] // GROUP
    half, head_dim = last.shape[0], keys_ref.shape[1]
    at = 0
    order = row_order(place_ref[1], count)
    for start, size in order[:-2]:
        keys_ref[pl.ds(start, size), :] = first_ref[at : at + size, :]
        at += size
    for (start, size), ref in zip(order[-2:], (last, last_other), strict=True):
        keys_ref[pl.ds(start, size), :] = jnp.dot(ref[...], weights[...], preferred_element_type=F32)
    states = []
    for off in range(GROUP):
        span = slice(off * count, (off + 1) * count)
        values = all_ref[span, head_dim : 2 * head_dim]
        states.append(dot3(split(values.T), split(keys_ref[span, :])))
    group_sums(place_ref[0], states, sums_ref, total_ref, False)


def inner_rest(scale, all_ref, keys_ref, grad_ref, value_ref, state_ref):
    width = keys_ref.shape[1]
    count = keys_ref.shape[0] // GROUP
    places = lax.broadcasted_iota(jnp.int32, (count, count), 0)
    others = lax.broadcasted_iota(jnp.int32, (count, count), 1)
    for off in range(GROUP):
        span = slice(off * count, (off + 1) * count)
        rows = all_ref[span, :]
        lifted, values, dout = (split(part(rows, k, width)) for k in range(3))
        keys = split(keys_ref[span, :])
        mixed = jnp.where(others >= places, dot3(keys, lifted, True), 0.0)
        carried = dot3(keys, split(grad_ref[off * width : (off + 1) * width, :]), True)
        value_ref[span, :] = carried + scale * dot3(split(mixed), dout)
        scores = jnp.where(places >= others, dot3(dout, values, True), 0.0)
        state_ref[span, :] = dot3(split(scores), keys)


def results(all_ref, sums_ref, before_ref, state_ref, value_ref, own, near, far, both):
    width = before_ref.shape[1]
    count = state_ref.shape[0] // GROUP
    for off, ref in enumerate((own, near, far, both)):
        span = slice(off * count, (off + 1) * count)
        before = sums_ref[off * width : (off + 1) * width, :] + before_ref[...]
        state = state_ref[span, :] + dot3(split(all_ref[span, 2 * width :]), split(before))
        ref[:, :width] = state.astype(ref.dtype)
        ref[:, width:] = value_ref[span, :].astype(ref.dtype)


def at_home(scale, place_ref, q_ref, routing_ref, gates_ref, own, near, far, both, query_ref, value_ref, gate_ref):
    queries, routing, gates = q_ref[...], routing_ref[...].T, gates_ref[...].T
    width = queries.shape[1]
    query = jnp.zeros_like(queries)
    value = jnp.zeros_like(queries)
    gate = jnp.zeros(gate_ref.shape[::-1], F32)
    for off, ref in enumerate((own, near, far, both)):
        hit = routing == (place_ref[0] ^ off)
        weight = jnp.sum(jnp.where(hit, gates, 0.0), axis=1, keepdims=True)
        routed = jnp.sum(hit.astype(F32), axis=1, keepdims=True)
        state = ref[:, :width].astype(F32)
        query = query + weight * state
        value = value + routed * ref[:, width:].astype(F32)
        gate = gate + jnp.where(hit, jnp.sum(queries * state, axis=1, keepdims=True), 0.0)
    query_ref[...] = scale * query
    value_ref[...] = value
    gate_ref[...] = (scale * gate).T


def by_column(place_ref, x_ref, own, near, far, both):
    size = own.shape[1]
    for off, ref in enumerate((own, near, far, both)):
        ref[...] = x_ref[:, pl.ds(pl.multiple_of((place_ref[0] ^ off) * size, size), size)]


def by_row(place_ref, *refs):
    parts, (own, near, far, both, room) = refs[:-5], refs[-5:]
    size = own.shape[0]
    total = parts[0][...]
    for ref in parts[1:]:
        total = total + ref[...].astype(F32)
    room[...] = total
    for off, ref in enumerate((own, near, far, both)):
        ref[...] = room[pl.ds(pl.multiple_of((place_ref[0] ^ off) * size, size), size), :]


def in_columns(place_ref, own, near, far, both, out_ref):
    size = own.shape[1]
    for off, ref in enumerate((own, near, far, both)):
        out_ref[:, pl.ds(pl.multiple_of((place_ref[0] ^ off) * size, size), size)] = ref[...]


def swap(x, off, parts):
    return lax.ppermute(x, "ctx", [(i, i ^ off) for i in range(parts)])


def other_core(x):
    return lax.ppermute(x, "head", [(i, i ^ 1) for i in range(lax.axis_size("head"))])


def from_groups(total, steps, parts):
    return [swap(total, off, parts) for off in steps[1:]]


def prefix(total, got, steps, here, reverse):
    before = jnp.zeros_like(total)
    for off, x in zip(steps[1:], got, strict=True):
        other = here ^ off
        before = before + jnp.where(other > here if reverse else other < here, x, 0.0)
    return before


def over_heads(x):
    count = lax.axis_size("head")
    bit = 1
    while bit < count:
        x = x + lax.ppermute(x, "head", [(i, i ^ bit) for i in range(count)])
        bit *= 2
    return x


def on_device(tokens, queries, values, dout, key_weight, routing, gates):
    count, width = tokens.shape
    rows, memories, head_dim = key_weight.shape
    parts = lax.axis_size("ctx")
    steps = list(range(0, parts, GROUP))
    here = lax.axis_index("ctx").astype(jnp.int32)
    core = lax.axis_index("head").astype(jnp.int32) & 1
    at = jnp.stack([here & (GROUP - 1), core, here // GROUP, here])
    scale = 1.0 / math.sqrt(head_dim * count * parts)
    tall = GROUP * count
    smem = pl.BlockSpec(memory_space=pltpu.SMEM)
    vmem = pl.BlockSpec(memory_space=pltpu.VMEM)
    anywhere = pl.BlockSpec(memory_space=pl.ANY)

    def shape(r, c, dtype=F32):
        return jax.ShapeDtypeStruct((r, c), dtype)

    def stack(*blocks, waits=()):
        size = sum(x.shape[0] for x in blocks)
        return call(
            pack,
            shape(size, blocks[0].shape[1], blocks[0].dtype),
            *blocks,
            spaces=[anywhere] * len(blocks),
            scratch=[pltpu.SemaphoreType.DMA((len(blocks),))],
            waits=waits,
        )

    half = lax.dynamic_slice(tokens, (core * (count // 2), jnp.int32(0)), (count // 2, width))
    from_x, from_y = swap(half, 1, parts), swap(half, 2, parts)

    mine = call(
        by_column,
        [shape(rows, head_dim, BF16)] * 4,
        at, key_weight.reshape(rows, memories * head_dim),
        spaces=[smem, vmem],
    )
    weights = [mine[0]] + [swap(mine[off], off, parts) for off in (1, 2, 3)]

    sent = call(
        messages,
        [shape(count, 3 * head_dim)] + [shape(count + TAIL, 3 * head_dim)] * 3,
        at, queries, values, dout, routing.T, gates.T,
        spaces=[smem] + [anywhere] * 5,
        scratch=[pltpu.VMEM((count, head_dim), F32)] * 3
        + [pltpu.VMEM(x.shape[::-1], x.dtype) for x in (routing, gates)]
        + [pltpu.SemaphoreType.DMA((5,))],
    )
    coded = [x.astype(F16) for x in sent[1:]]
    got = [swap(x, off, parts).astype(F32) for off, x in zip((1, 2, 3), coded)]

    neighbours = stack(from_x, from_y, waits=(*sent[1:], *weights))
    neighbours_other = other_core(neighbours)

    block = stack(*weights, waits=sent[1:])
    chunks, layout, held = [block], [list(range(GROUP))], list(range(GROUP))
    bit = parts // 2
    while bit >= GROUP:
        other = swap(block, bit, parts)
        chunks.append(other)
        layout.append([off ^ bit for off in held])
        held = held + layout[-1]
        if bit > GROUP:
            block = stack(block, other)
        bit //= 2

    quarter = count // 4
    last_a, last_b = call(
        cut,
        [shape(quarter, width, BF16)] * 2,
        from_x, from_y,
        spaces=[anywhere] * 2,
        scratch=[pltpu.SemaphoreType.DMA((2,))],
        waits=(*got, neighbours_other),
    )
    last_a, last_b = swap(last_a, 2, parts), swap(last_b, 1, parts)

    every, grad_sums, total = call(
        functools.partial(grad_states, scale),
        [shape(tall, 3 * head_dim), shape(GROUP * head_dim, head_dim), shape(head_dim, head_dim)],
        at, sent[0], *got,
        spaces=[smem] + [vmem] * 4,
        waits=(neighbours_other,),
        flops=6 * tall * head_dim * head_dim,
    )
    totals = from_groups(total, steps, parts)
    before = prefix(total, totals, steps, here, True)
    inner_k = call(
        functools.partial(inner_key, scale),
        shape(tall, head_dim),
        every,
        flops=12 * tall * count * head_dim,
    )
    low, grad_in = call(
        key_low,
        [shape(tall, head_dim, BF16), shape(GROUP * head_dim, head_dim)],
        every, grad_sums, before, inner_k,
        flops=6 * tall * head_dim * head_dim,
    )

    first, weights = call(
        functools.partial(first_keys, layout, parts),
        [shape(3 * count, head_dim), shape(width, head_dim, BF16)],
        at, *chunks, tokens, neighbours, neighbours_other,
        spaces=[smem] + [vmem] * (3 + len(chunks)),
        waits=(inner_k,),
        flops=2 * tall * width * head_dim,
    )
    product, last_low = call(
        first_products,
        [shape(head_dim, width), shape(head_dim, count, BF16)],
        at, tokens, neighbours, neighbours_other, low,
        spaces=[smem] + [vmem] * 4,
        scratch=[pltpu.VMEM((tall, head_dim), BF16)],
        flops=2 * tall * width * head_dim,
    )
    last = stack(last_a, last_b, waits=(first, *totals))
    last_other = other_core(last)

    keys, sums, key_total = call(
        key_states,
        [shape(tall, head_dim), shape(GROUP * head_dim, head_dim), shape(head_dim, head_dim)],
        at, first, weights, last, last_other, every,
        spaces=[smem] + [vmem] * 5,
        flops=2 * count * width * head_dim,
    )
    key_totals = from_groups(key_total, steps, parts)

    span = width // len(steps)
    sent = call(
        functools.partial(products, steps),
        [shape(span, head_dim)] + [shape(span, head_dim, BF16)] * (len(steps) - 1),
        at, product, last_low, last, last_other,
        spaces=[smem] + [vmem] * 4,
        waits=(key_total,),
        scratch=[pltpu.VMEM((head_dim, width), F32)],
        flops=2 * count * width * head_dim,
    )
    parts_of_sum = [sent[0]] + [swap(x, off, parts) for off, x in zip(steps[1:], sent[1:], strict=True)]
    inner_v, inner_state = call(
        functools.partial(inner_rest, scale),
        [shape(tall, head_dim)] * 2,
        every, keys, grad_in,
        waits=(sent[0],),
        flops=24 * tall * count * head_dim,
    )

    mine = call(
        by_row,
        [shape(rows, head_dim)] * 4,
        at, *parts_of_sum,
        spaces=[smem] + [vmem] * len(steps),
        scratch=[pltpu.VMEM((GROUP * rows, head_dim), F32)],
    )
    others = [swap(mine[off], off, parts) for off in (1, 2, 3)]

    before = prefix(key_total, key_totals, steps, here, False)
    sent = call(
        results,
        [shape(count, 2 * head_dim)] + [shape(count, 2 * head_dim, BF16)] * 3,
        every, sums, before, inner_state, inner_v,
        flops=6 * tall * head_dim * head_dim,
    )
    query_grad, value_grad, gate_part = call(
        functools.partial(at_home, scale),
        [shape(count, head_dim), shape(count, head_dim), shape(routing.shape[1], count)],
        at, queries, routing.T, gates.T, sent[0], *[swap(sent[off], off, parts) for off in (1, 2, 3)],
        spaces=[smem] + [vmem] * 7,
        waits=mine,
    )
    gate_grad = over_heads(gate_part).T
    key_grad = call(
        in_columns,
        shape(rows, memories * head_dim),
        at, mine[0], *others,
        spaces=[smem] + [vmem] * 4,
    ).reshape(rows, memories, head_dim)
    return (key_grad, query_grad, value_grad, gate_grad)


def solution(mesh):
    return jax.shard_map(
        on_device,
        mesh=mesh,
        in_specs=(
            P("ctx", None),
            P("ctx", "head"),
            P("ctx", "head"),
            P("ctx", "head"),
            P("ctx", None, "head"),
            P("ctx", None),
            P("ctx", None),
        ),
        out_specs=(P("ctx", None, "head"), P("ctx", "head"), P("ctx", "head"), P("ctx", None)),
        check_vma=False,
    )
```

```python
import functools
import math

import jax
import jax.numpy as jnp
from jax import lax
from jax.experimental import pallas as pl
from jax.experimental.pallas import tpu as pltpu
from jax.sharding import PartitionSpec as P

F32 = jnp.float32
BF16 = jnp.bfloat16
F16 = jnp.float16
GROUP = 4
TAIL = 16


def split(x):
    high = x.astype(BF16)
    return high, (x - high.astype(F32)).astype(BF16)


def dot3(a, b, b_last=False):
    side = 1 if b_last else 0
    left = jnp.concatenate([a[0], a[0], a[1]], axis=1)
    right = jnp.concatenate([b[0], b[1], b[0]], axis=side)
    return lax.dot_general(left, right, (((1,), (side,)), ((), ())), preferred_element_type=F32)


def part(x, k, width):
    return x[:, k * width : (k + 1) * width]


def call(body, outs, *args, scratch=(), spaces=None, flops=0, waits=()):
    vmem = pl.BlockSpec(memory_space=pltpu.VMEM)
    size = sum(a.size * a.dtype.itemsize for a in args)
    count = len(args)

    def kernel(*refs):
        body(*refs[:count], *refs[count + len(waits) :])

    return pl.pallas_call(
        kernel,
        out_shape=outs,
        in_specs=([vmem] * count if spaces is None else spaces) + [pl.BlockSpec(memory_space=pl.ANY)] * len(waits),
        out_specs=jax.tree.map(lambda _: vmem, outs),
        scratch_shapes=list(scratch),
        cost_estimate=pl.CostEstimate(flops=flops, bytes_accessed=size, transcendentals=0),
        compiler_params=pltpu.CompilerParams(vmem_limit_bytes=20 * 1024 * 1024),
    )(*args, *waits)


def exponent(x):
    top = jnp.max(jnp.abs(x), axis=(0, 1), keepdims=True)
    return jnp.clip(jnp.ceil(jnp.log(jnp.maximum(top, 1e-30)) * (1.0 / math.log(2.0))), -90.0, 40.0) - 14.0


def power(k):
    return jnp.exp(k * math.log(2.0))


def fetch(refs, rooms, sem):
    copies = [pltpu.make_async_copy(ref, room, sem.at[k]) for k, (ref, room) in enumerate(zip(refs, rooms, strict=True))]
    for copy in copies:
        copy.start()
    for copy in copies:
        copy.wait()


def router_columns(place, routing, gates):
    hits = [routing == (place ^ off) for off in range(GROUP)]
    rows = [jnp.sum(jnp.where(hit, gates, 0.0), axis=0, keepdims=True) for hit in hits]
    rows += [jnp.sum(hit.astype(F32), axis=0, keepdims=True) for hit in hits]
    columns = jnp.concatenate(rows, axis=0).T
    return [(columns[:, off : off + 1], columns[:, GROUP + off : GROUP + off + 1], hit) for off, hit in enumerate(hits)]


def messages(place_ref, q_at, v_at, dout_at, routing_at, gates_at, own, near, far, both, q_ref, v_ref, dout_ref, routing_ref, gates_ref, sem):
    fetch((q_at, v_at, dout_at, routing_at, gates_at), (q_ref, v_ref, dout_ref, routing_ref, gates_ref), sem)
    count, width = q_ref.shape
    routers = router_columns(place_ref[0], routing_ref[...], gates_ref[...])
    q, v, dout = q_ref[...], v_ref[...], dout_ref[...]
    exponents = [exponent(x) for x in (q, v, dout)]
    scales = [1.0 / power(k) for k in exponents]
    for off, ref in enumerate((own, near, far, both)):
        weight, routed, _ = routers[off]
        for k, x in enumerate((weight * q, routed * v, dout)):
            column = slice(k * width, (k + 1) * width)
            if off:
                ref[:count, column] = x * scales[k]
                ref[count:, column] = jnp.broadcast_to(exponents[k], (TAIL, width))
            else:
                ref[:, column] = x


def group_sums(place, states, sums_ref, total_ref, reverse):
    size = states[0].shape[0]
    for to in range(GROUP):
        total = jnp.zeros_like(states[0])
        for off in range(GROUP):
            counts = (place ^ off) > (place ^ to) if reverse else (place ^ off) < (place ^ to)
            total = total + jnp.where(counts, states[off], 0.0)
        sums_ref[to * size : (to + 1) * size, :] = total
    total_ref[...] = (states[0] + states[1]) + (states[2] + states[3])


def grad_states(scale, place_ref, own, near, far, both, all_ref, sums_ref, total_ref):
    count = own.shape[0]
    width = own.shape[1] // 3
    states = []
    for off, ref in enumerate((own, near, far, both)):
        for k in range(3):
            column = slice(k * width, (k + 1) * width)
            x = ref[:count, column]
            if off:
                x = x * power(ref[count : count + 1, column])
            all_ref[off * count : (off + 1) * count, column] = x
        rows = all_ref[off * count : (off + 1) * count, :]
        states.append(scale * dot3(split(part(rows, 2, width).T), split(part(rows, 0, width))))
    group_sums(place_ref[0], states, sums_ref, total_ref, True)


def inner_key(scale, all_ref, out_ref):
    width = all_ref.shape[1] // 3
    count = all_ref.shape[0] // GROUP
    places = lax.broadcasted_iota(jnp.int32, (count, count), 0)
    others = lax.broadcasted_iota(jnp.int32, (count, count), 1)
    for off in range(GROUP):
        rows = all_ref[off * count : (off + 1) * count, :]
        scores = dot3(split(part(rows, 1, width)), split(part(rows, 2, width)), True)
        scores = jnp.where(others >= places, scores, 0.0)
        out_ref[off * count : (off + 1) * count, :] = scale * dot3(split(scores), split(part(rows, 0, width)))


def key_low(all_ref, sums_ref, before_ref, inner_ref, low_ref, grad_ref):
    width = all_ref.shape[1] // 3
    count = all_ref.shape[0] // GROUP
    for off in range(GROUP):
        grad = sums_ref[off * width : (off + 1) * width, :] + before_ref[...]
        grad_ref[off * width : (off + 1) * width, :] = grad
        span = slice(off * count, (off + 1) * count)
        carried = dot3(split(all_ref[span, width : 2 * width]), split(grad))
        low_ref[span, :] = (carried + inner_ref[span, :]).astype(BF16)


def pack(*refs):
    sources, out_ref, sem = refs[:-2], refs[-2], refs[-1]
    copies, at = [], 0
    for k, ref in enumerate(sources):
        copies.append(pltpu.make_async_copy(ref, out_ref.at[pl.ds(at, ref.shape[0]), :], sem.at[k]))
        at += ref.shape[0]
    for copy in copies:
        copy.start()
    for copy in copies:
        copy.wait()


def cut(x_ref, y_ref, a_ref, b_ref, sem):
    size = a_ref.shape[0]
    copies = [
        pltpu.make_async_copy(x_ref.at[pl.ds(0, size), :], a_ref, sem.at[0]),
        pltpu.make_async_copy(y_ref.at[pl.ds(size, size), :], b_ref, sem.at[1]),
    ]
    for copy in copies:
        copy.start()
    for copy in copies:
        copy.wait()


def row_order(core, count):
    half = count // 2
    found = [(0, 0, count)]
    for whose in (core, 1 - core):
        for block in (1, 2):
            found.append((block, whose * half, half))
    for whose in (core, 1 - core):
        found.append((3, whose * half, half))
    return [
        (pl.multiple_of(block * count + row, size), size) if block else (0, size) for block, row, size in found
    ]


def first_products(place_ref, own, mine, other, low_ref, out_ref, last_low_ref, room):
    at = 0
    for start, size in row_order(place_ref[1], own.shape[0]):
        room[at : at + size, :] = low_ref[pl.ds(start, size), :]
        at += size
    low = room[...].T
    at, total = 0, None
    for ref in (own, mine, other):
        term = jnp.dot(low[:, at : at + ref.shape[0]], ref[...], preferred_element_type=F32)
        total = term if total is None else total + term
        at += ref.shape[0]
    out_ref[...] = total
    last_low_ref[...] = low[:, at:]


def products(steps, place_ref, first_ref, low_ref, last, last_other, *refs):
    outs, turned = refs[:-1], refs[-1]
    half, width = last.shape
    turned[...] = first_ref[...] + (
        jnp.dot(low_ref[:, :half], last[...], preferred_element_type=F32)
        + jnp.dot(low_ref[:, half:], last_other[...], preferred_element_type=F32)
    )
    group = place_ref[2]
    span = width // len(steps)
    for off, ref in zip(steps, outs, strict=True):
        start = pl.multiple_of((group ^ off // GROUP) * span, span)
        ref[...] = turned[:, pl.ds(start, span)].T.astype(ref.dtype)


def first_keys(layout, parts, place_ref, *refs):
    chunks = len(layout)
    own, mine, other, keys_ref, weights = refs[chunks:]
    rows = weights.shape[0] // parts
    here = place_ref[3]
    for ref, offsets in zip(refs[:chunks], layout, strict=True):
        for k, off in enumerate(offsets):
            start = pl.multiple_of((here ^ off) * rows, rows)
            weights[pl.ds(start, rows), :] = ref[k * rows : (k + 1) * rows, :]
    at = 0
    for ref in (own, mine, other):
        keys_ref[at : at + ref.shape[0], :] = jnp.dot(ref[...], weights[...], preferred_element_type=F32)
        at += ref.shape[0]


def key_states(place_ref, first_ref, weights, last, last_other, all_ref, keys_ref, sums_ref, total_ref):
    count = all_ref.shape[0] // GROUP
    half, head_dim = last.shape[0], keys_ref.shape[1]
    at = 0
    order = row_order(place_ref[1], count)
    for start, size in order[:-2]:
        keys_ref[pl.ds(start, size), :] = first_ref[at : at + size, :]
        at += size
    for (start, size), ref in zip(order[-2:], (last, last_other), strict=True):
        keys_ref[pl.ds(start, size), :] = jnp.dot(ref[...], weights[...], preferred_element_type=F32)
    states = []
    for off in range(GROUP):
        span = slice(off * count, (off + 1) * count)
        values = all_ref[span, head_dim : 2 * head_dim]
        states.append(dot3(split(values.T), split(keys_ref[span, :])))
    group_sums(place_ref[0], states, sums_ref, total_ref, False)


def inner_rest(scale, all_ref, keys_ref, grad_ref, value_ref, state_ref):
    width = keys_ref.shape[1]
    count = keys_ref.shape[0] // GROUP
    places = lax.broadcasted_iota(jnp.int32, (count, count), 0)
    others = lax.broadcasted_iota(jnp.int32, (count, count), 1)
    for off in range(GROUP):
        span = slice(off * count, (off + 1) * count)
        rows = all_ref[span, :]
        lifted, values, dout = (split(part(rows, k, width)) for k in range(3))
        keys = split(keys_ref[span, :])
        mixed = jnp.where(others >= places, dot3(keys, lifted, True), 0.0)
        carried = dot3(keys, split(grad_ref[off * width : (off + 1) * width, :]), True)
        value_ref[span, :] = carried + scale * dot3(split(mixed), dout)
        scores = jnp.where(places >= others, dot3(dout, values, True), 0.0)
        state_ref[span, :] = dot3(split(scores), keys)


def results(all_ref, sums_ref, before_ref, state_ref, value_ref, own, near, far, both):
    width = before_ref.shape[1]
    count = state_ref.shape[0] // GROUP
    for off, ref in enumerate((own, near, far, both)):
        span = slice(off * count, (off + 1) * count)
        before = sums_ref[off * width : (off + 1) * width, :] + before_ref[...]
        state = state_ref[span, :] + dot3(split(all_ref[span, 2 * width :]), split(before))
        ref[:, :width] = state.astype(ref.dtype)
        ref[:, width:] = value_ref[span, :].astype(ref.dtype)


def at_home(scale, place_ref, q_ref, routing_ref, gates_ref, own, near, far, both, query_ref, value_ref, gate_ref):
    queries = q_ref[...]
    width = queries.shape[1]
    query = jnp.zeros_like(queries)
    value = jnp.zeros_like(queries)
    gate = jnp.zeros(gate_ref.shape, F32)
    ones = jnp.ones((gate.shape[0], 2 * width), BF16)
    routers = router_columns(place_ref[0], routing_ref[...], gates_ref[...])
    for (weight, routed, hit), ref in zip(routers, (own, near, far, both), strict=True):
        state = ref[:, :width].astype(F32)
        query = query + weight * state
        value = value + routed * ref[:, width:].astype(F32)
        terms = jnp.concatenate(split(queries * state), axis=1)
        mine = lax.dot_general(ones, terms, (((1,), (1,)), ((), ())), preferred_element_type=F32)
        gate = gate + jnp.where(hit, mine, 0.0)
    query_ref[...] = scale * query
    value_ref[...] = value
    gate_ref[...] = scale * gate


def by_column(place_ref, x_ref, own, near, far, both):
    size = own.shape[1]
    for off, ref in enumerate((own, near, far, both)):
        ref[...] = x_ref[:, pl.ds(pl.multiple_of((place_ref[0] ^ off) * size, size), size)]


def by_row(place_ref, *refs):
    parts, (own, near, far, both, room) = refs[:-5], refs[-5:]
    size = own.shape[0]
    total = parts[0][...]
    for ref in parts[1:]:
        total = total + ref[...].astype(F32)
    room[...] = total
    for off, ref in enumerate((own, near, far, both)):
        ref[...] = room[pl.ds(pl.multiple_of((place_ref[0] ^ off) * size, size), size), :]


def in_columns(place_ref, own, near, far, both, out_ref):
    size = own.shape[1]
    for off, ref in enumerate((own, near, far, both)):
        out_ref[:, pl.ds(pl.multiple_of((place_ref[0] ^ off) * size, size), size)] = ref[...]


def swap(x, off, parts):
    return lax.ppermute(x, "ctx", [(i, i ^ off) for i in range(parts)])


def other_core(x):
    return lax.ppermute(x, "head", [(i, i ^ 1) for i in range(lax.axis_size("head"))])


def from_groups(total, steps, parts):
    return [swap(total, off, parts) for off in steps[1:]]


def prefix(total, got, steps, here, reverse):
    before = jnp.zeros_like(total)
    for off, x in zip(steps[1:], got, strict=True):
        other = here ^ off
        before = before + jnp.where(other > here if reverse else other < here, x, 0.0)
    return before


def over_heads(x):
    count = lax.axis_size("head")
    bit = 1
    while bit < count:
        x = x + lax.ppermute(x, "head", [(i, i ^ bit) for i in range(count)])
        bit *= 2
    return x


def on_device(tokens, queries, values, dout, key_weight, routing, gates):
    count, width = tokens.shape
    rows, memories, head_dim = key_weight.shape
    parts = lax.axis_size("ctx")
    steps = list(range(0, parts, GROUP))
    here = lax.axis_index("ctx").astype(jnp.int32)
    core = lax.axis_index("head").astype(jnp.int32) & 1
    at = jnp.stack([here & (GROUP - 1), core, here // GROUP, here])
    scale = 1.0 / math.sqrt(head_dim * count * parts)
    tall = GROUP * count
    smem = pl.BlockSpec(memory_space=pltpu.SMEM)
    vmem = pl.BlockSpec(memory_space=pltpu.VMEM)
    anywhere = pl.BlockSpec(memory_space=pl.ANY)

    def shape(r, c, dtype=F32):
        return jax.ShapeDtypeStruct((r, c), dtype)

    def stack(*blocks, waits=()):
        size = sum(x.shape[0] for x in blocks)
        return call(
            pack,
            shape(size, blocks[0].shape[1], blocks[0].dtype),
            *blocks,
            spaces=[anywhere] * len(blocks),
            scratch=[pltpu.SemaphoreType.DMA((len(blocks),))],
            waits=waits,
        )

    half = lax.dynamic_slice(tokens, (core * (count // 2), jnp.int32(0)), (count // 2, width))
    from_x, from_y = swap(half, 1, parts), swap(half, 2, parts)

    mine = call(
        by_column,
        [shape(rows, head_dim, BF16)] * 4,
        at, key_weight.reshape(rows, memories * head_dim),
        spaces=[smem, vmem],
    )
    weights = [mine[0]] + [swap(mine[off], off, parts) for off in (1, 2, 3)]

    sent = call(
        messages,
        [shape(count, 3 * head_dim)] + [shape(count + TAIL, 3 * head_dim)] * 3,
        at, queries, values, dout, routing.T, gates.T,
        spaces=[smem] + [anywhere] * 5,
        scratch=[pltpu.VMEM((count, head_dim), F32)] * 3
        + [pltpu.VMEM(x.shape[::-1], x.dtype) for x in (routing, gates)]
        + [pltpu.SemaphoreType.DMA((5,))],
    )
    coded = [x.astype(F16) for x in sent[1:]]
    got = [swap(x, off, parts).astype(F32) for off, x in zip((1, 2, 3), coded)]

    neighbours = stack(from_x, from_y, waits=(*sent[1:], *weights))
    neighbours_other = other_core(neighbours)

    block = stack(*weights, waits=sent[1:])
    chunks, layout, held = [block], [list(range(GROUP))], list(range(GROUP))
    bit = parts // 2
    while bit >= GROUP:
        other = swap(block, bit, parts)
        chunks.append(other)
        layout.append([off ^ bit for off in held])
        held = held + layout[-1]
        if bit > GROUP:
            block = stack(block, other)
        bit //= 2

    quarter = count // 4
    last_a, last_b = call(
        cut,
        [shape(quarter, width, BF16)] * 2,
        from_x, from_y,
        spaces=[anywhere] * 2,
        scratch=[pltpu.SemaphoreType.DMA((2,))],
        waits=(*got, neighbours_other),
    )
    last_a, last_b = swap(last_a, 2, parts), swap(last_b, 1, parts)

    every, grad_sums, total = call(
        functools.partial(grad_states, scale),
        [shape(tall, 3 * head_dim), shape(GROUP * head_dim, head_dim), shape(head_dim, head_dim)],
        at, sent[0], *got,
        spaces=[smem] + [vmem] * 4,
        waits=(neighbours_other,),
        flops=6 * tall * head_dim * head_dim,
    )
    totals = from_groups(total, steps, parts)
    before = prefix(total, totals, steps, here, True)
    inner_k = call(
        functools.partial(inner_key, scale),
        shape(tall, head_dim),
        every,
        flops=12 * tall * count * head_dim,
    )
    low, grad_in = call(
        key_low,
        [shape(tall, head_dim, BF16), shape(GROUP * head_dim, head_dim)],
        every, grad_sums, before, inner_k,
        flops=6 * tall * head_dim * head_dim,
    )

    first, weights = call(
        functools.partial(first_keys, layout, parts),
        [shape(3 * count, head_dim), shape(width, head_dim, BF16)],
        at, *chunks, tokens, neighbours, neighbours_other,
        spaces=[smem] + [vmem] * (3 + len(chunks)),
        waits=(inner_k,),
        flops=2 * tall * width * head_dim,
    )
    product, last_low = call(
        first_products,
        [shape(head_dim, width), shape(head_dim, count, BF16)],
        at, tokens, neighbours, neighbours_other, low,
        spaces=[smem] + [vmem] * 4,
        scratch=[pltpu.VMEM((tall, head_dim), BF16)],
        flops=2 * tall * width * head_dim,
    )
    last = stack(last_a, last_b, waits=(first[:8], *totals))
    last_other = other_core(last)

    keys, sums, key_total = call(
        key_states,
        [shape(tall, head_dim), shape(GROUP * head_dim, head_dim), shape(head_dim, head_dim)],
        at, first, weights, last, last_other, every,
        spaces=[smem] + [vmem] * 5,
        flops=2 * count * width * head_dim,
    )
    key_totals = from_groups(key_total, steps, parts)

    span = width // len(steps)
    sent = call(
        functools.partial(products, steps),
        [shape(span, head_dim)] + [shape(span, head_dim, BF16)] * (len(steps) - 1),
        at, product, last_low, last, last_other,
        spaces=[smem] + [vmem] * 4,
        waits=(key_total,),
        scratch=[pltpu.VMEM((head_dim, width), F32)],
        flops=2 * count * width * head_dim,
    )
    parts_of_sum = [sent[0]] + [swap(x, off, parts) for off, x in zip(steps[1:], sent[1:], strict=True)]
    inner_v, inner_state = call(
        functools.partial(inner_rest, scale),
        [shape(tall, head_dim)] * 2,
        every, keys, grad_in,
        waits=(sent[0],),
        flops=24 * tall * count * head_dim,
    )

    mine = call(
        by_row,
        [shape(rows, head_dim)] * 4,
        at, *parts_of_sum,
        spaces=[smem] + [vmem] * len(steps),
        scratch=[pltpu.VMEM((GROUP * rows, head_dim), F32)],
    )
    others = [swap(mine[off], off, parts) for off in (1, 2, 3)]

    before = prefix(key_total, key_totals, steps, here, False)
    sent = call(
        results,
        [shape(count, 2 * head_dim)] + [shape(count, 2 * head_dim, BF16)] * 3,
        every, sums, before, inner_state, inner_v,
        flops=6 * tall * head_dim * head_dim,
    )
    query_grad, value_grad, gate_part = call(
        functools.partial(at_home, scale),
        [shape(count, head_dim), shape(count, head_dim), shape(routing.shape[1], count)],
        at, queries, routing.T, gates.T, sent[0], *[swap(sent[off], off, parts) for off in (1, 2, 3)],
        spaces=[smem] + [vmem] * 7,
        waits=mine,
    )
    gate_grad = over_heads(gate_part).T
    key_grad = call(
        in_columns,
        shape(rows, memories * head_dim),
        at, mine[0], *others,
        spaces=[smem] + [vmem] * 4,
    ).reshape(rows, memories, head_dim)
    return (key_grad, query_grad, value_grad, gate_grad)


def solution(mesh):
    return jax.shard_map(
        on_device,
        mesh=mesh,
        in_specs=(
            P("ctx", None),
            P("ctx", "head"),
            P("ctx", "head"),
            P("ctx", "head"),
            P("ctx", None, "head"),
            P("ctx", None),
            P("ctx", None),
        ),
        out_specs=(P("ctx", None, "head"), P("ctx", "head"), P("ctx", "head"), P("ctx", None)),
        check_vma=False,
    )
```

```python
import functools
import math

import jax
import jax.numpy as jnp
from jax import lax
from jax.experimental import pallas as pl
from jax.experimental.pallas import tpu as pltpu
from jax.sharding import PartitionSpec as P

F32 = jnp.float32
BF16 = jnp.bfloat16
F16 = jnp.float16
GROUP = 4
TAIL = 16


def split(x):
    high = x.astype(BF16)
    return high, (x - high.astype(F32)).astype(BF16)


def dot3(a, b, b_last=False):
    side = 1 if b_last else 0
    left = jnp.concatenate([a[0], a[0], a[1]], axis=1)
    right = jnp.concatenate([b[0], b[1], b[0]], axis=side)
    return lax.dot_general(left, right, (((1,), (side,)), ((), ())), preferred_element_type=F32)


def part(x, k, width):
    return x[:, k * width : (k + 1) * width]


def call(body, outs, *args, scratch=(), spaces=None, flops=0, waits=()):
    vmem = pl.BlockSpec(memory_space=pltpu.VMEM)
    size = sum(a.size * a.dtype.itemsize for a in args)
    count = len(args)

    def kernel(*refs):
        body(*refs[:count], *refs[count + len(waits) :])

    return pl.pallas_call(
        kernel,
        out_shape=outs,
        in_specs=([vmem] * count if spaces is None else spaces) + [pl.BlockSpec(memory_space=pl.ANY)] * len(waits),
        out_specs=jax.tree.map(lambda _: vmem, outs),
        scratch_shapes=list(scratch),
        cost_estimate=pl.CostEstimate(flops=flops, bytes_accessed=size, transcendentals=0),
        compiler_params=pltpu.CompilerParams(vmem_limit_bytes=20 * 1024 * 1024),
    )(*args, *waits)


def exponent(x):
    top = jnp.max(jnp.abs(x), axis=(0, 1), keepdims=True)
    return jnp.clip(jnp.ceil(jnp.log(jnp.maximum(top, 1e-30)) * (1.0 / math.log(2.0))), -90.0, 40.0) - 14.0


def power(k):
    return jnp.exp(k * math.log(2.0))


def fetch(refs, rooms, sem):
    copies = [pltpu.make_async_copy(ref, room, sem.at[k]) for k, (ref, room) in enumerate(zip(refs, rooms, strict=True))]
    for copy in copies:
        copy.start()
    for copy in copies:
        copy.wait()


def router_columns(place, routing, gates):
    hits = [routing == (place ^ off) for off in range(GROUP)]
    rows = [jnp.sum(jnp.where(hit, gates, 0.0), axis=0, keepdims=True) for hit in hits]
    rows += [jnp.sum(hit.astype(F32), axis=0, keepdims=True) for hit in hits]
    columns = jnp.concatenate(rows, axis=0).T
    return [(columns[:, off : off + 1], columns[:, GROUP + off : GROUP + off + 1], hit) for off, hit in enumerate(hits)]


def messages(place_ref, q_at, v_at, dout_at, routing_at, gates_at, own, near, far, both, q_ref, v_ref, dout_ref, routing_ref, gates_ref, sem):
    fetch((q_at, v_at, dout_at, routing_at, gates_at), (q_ref, v_ref, dout_ref, routing_ref, gates_ref), sem)
    count, width = q_ref.shape
    routers = router_columns(place_ref[0], routing_ref[...], gates_ref[...])
    q, v, dout = q_ref[...], v_ref[...], dout_ref[...]
    exponents = [exponent(x) for x in (q, v, dout)]
    scales = [1.0 / power(k) for k in exponents]
    for off, ref in enumerate((own, near, far, both)):
        weight, routed, _ = routers[off]
        for k, x in enumerate((weight * q, routed * v, dout)):
            column = slice(k * width, (k + 1) * width)
            if off:
                ref[:count, column] = x * scales[k]
                ref[count:, column] = jnp.broadcast_to(exponents[k], (TAIL, width))
            else:
                ref[:, column] = x


def group_sums(place, states, sums_ref, total_ref, reverse):
    size = states[0].shape[0]
    for to in range(GROUP):
        total = jnp.zeros_like(states[0])
        for off in range(GROUP):
            counts = (place ^ off) > (place ^ to) if reverse else (place ^ off) < (place ^ to)
            total = total + jnp.where(counts, states[off], 0.0)
        sums_ref[to * size : (to + 1) * size, :] = total
    total_ref[...] = (states[0] + states[1]) + (states[2] + states[3])


def grad_states(scale, place_ref, own, near, far, both, all_ref, sums_ref, total_ref):
    count = own.shape[0]
    width = own.shape[1] // 3
    states = []
    for off, ref in enumerate((own, near, far, both)):
        for k in range(3):
            column = slice(k * width, (k + 1) * width)
            x = ref[:count, column]
            if off:
                x = x * power(ref[count : count + 1, column])
            all_ref[off * count : (off + 1) * count, column] = x
        rows = all_ref[off * count : (off + 1) * count, :]
        states.append(scale * dot3(split(part(rows, 2, width).T), split(part(rows, 0, width))))
    group_sums(place_ref[0], states, sums_ref, total_ref, True)


def inner_key(scale, all_ref, out_ref):
    width = all_ref.shape[1] // 3
    count = all_ref.shape[0] // GROUP
    places = lax.broadcasted_iota(jnp.int32, (count, count), 0)
    others = lax.broadcasted_iota(jnp.int32, (count, count), 1)
    for off in range(GROUP):
        rows = all_ref[off * count : (off + 1) * count, :]
        scores = dot3(split(part(rows, 1, width)), split(part(rows, 2, width)), True)
        scores = jnp.where(others >= places, scores, 0.0)
        out_ref[off * count : (off + 1) * count, :] = scale * dot3(split(scores), split(part(rows, 0, width)))


def key_low(all_ref, sums_ref, before_ref, inner_ref, low_ref, grad_ref):
    width = all_ref.shape[1] // 3
    count = all_ref.shape[0] // GROUP
    for off in range(GROUP):
        grad = sums_ref[off * width : (off + 1) * width, :] + before_ref[...]
        grad_ref[off * width : (off + 1) * width, :] = grad
        span = slice(off * count, (off + 1) * count)
        carried = dot3(split(all_ref[span, width : 2 * width]), split(grad))
        low_ref[span, :] = (carried + inner_ref[span, :]).astype(BF16)


def pack(*refs):
    sources, out_ref, sem = refs[:-2], refs[-2], refs[-1]
    copies, at = [], 0
    for k, ref in enumerate(sources):
        copies.append(pltpu.make_async_copy(ref, out_ref.at[pl.ds(at, ref.shape[0]), :], sem.at[k]))
        at += ref.shape[0]
    for copy in copies:
        copy.start()
    for copy in copies:
        copy.wait()


def cut(x_ref, y_ref, a_ref, b_ref, sem):
    size = a_ref.shape[0]
    copies = [
        pltpu.make_async_copy(x_ref.at[pl.ds(0, size), :], a_ref, sem.at[0]),
        pltpu.make_async_copy(y_ref.at[pl.ds(size, size), :], b_ref, sem.at[1]),
    ]
    for copy in copies:
        copy.start()
    for copy in copies:
        copy.wait()


def row_order(core, count):
    half = count // 2
    found = [(0, 0, count)]
    for whose in (core, 1 - core):
        for block in (1, 2):
            found.append((block, whose * half, half))
    for whose in (core, 1 - core):
        found.append((3, whose * half, half))
    return [
        (pl.multiple_of(block * count + row, size), size) if block else (0, size) for block, row, size in found
    ]


def first_products(place_ref, own, mine, other, low_ref, out_ref, last_low_ref, room):
    at = 0
    for start, size in row_order(place_ref[1], own.shape[0]):
        room[at : at + size, :] = low_ref[pl.ds(start, size), :]
        at += size
    low = room[...].T
    at, total = 0, None
    for ref in (own, mine, other):
        term = jnp.dot(low[:, at : at + ref.shape[0]], ref[...], preferred_element_type=F32)
        total = term if total is None else total + term
        at += ref.shape[0]
    out_ref[...] = total
    last_low_ref[...] = low[:, at:]


def products(steps, place_ref, first_ref, low_ref, last, last_other, *refs):
    outs, turned = refs[:-1], refs[-1]
    half, width = last.shape
    turned[...] = first_ref[...] + (
        jnp.dot(low_ref[:, :half], last[...], preferred_element_type=F32)
        + jnp.dot(low_ref[:, half:], last_other[...], preferred_element_type=F32)
    )
    group = place_ref[2]
    span = width // len(steps)
    for off, ref in zip(steps, outs, strict=True):
        start = pl.multiple_of((group ^ off // GROUP) * span, span)
        ref[...] = turned[:, pl.ds(start, span)].T.astype(ref.dtype)


def first_keys(layout, parts, place_ref, *refs):
    chunks = len(layout)
    own, mine, other, keys_ref, weights = refs[chunks:]
    rows = weights.shape[0] // parts
    here = place_ref[3]
    for ref, offsets in zip(refs[:chunks], layout, strict=True):
        for k, off in enumerate(offsets):
            start = pl.multiple_of((here ^ off) * rows, rows)
            weights[pl.ds(start, rows), :] = ref[k * rows : (k + 1) * rows, :]
    at = 0
    for ref in (own, mine, other):
        keys_ref[at : at + ref.shape[0], :] = jnp.dot(ref[...], weights[...], preferred_element_type=F32)
        at += ref.shape[0]


def key_states(place_ref, first_ref, weights, last, last_other, all_ref, keys_ref, sums_ref, total_ref):
    count = all_ref.shape[0] // GROUP
    half, head_dim = last.shape[0], keys_ref.shape[1]
    at = 0
    order = row_order(place_ref[1], count)
    for start, size in order[:-2]:
        keys_ref[pl.ds(start, size), :] = first_ref[at : at + size, :]
        at += size
    for (start, size), ref in zip(order[-2:], (last, last_other), strict=True):
        keys_ref[pl.ds(start, size), :] = jnp.dot(ref[...], weights[...], preferred_element_type=F32)
    states = []
    for off in range(GROUP):
        span = slice(off * count, (off + 1) * count)
        values = all_ref[span, head_dim : 2 * head_dim]
        states.append(dot3(split(values.T), split(keys_ref[span, :])))
    group_sums(place_ref[0], states, sums_ref, total_ref, False)


def inner_rest(scale, all_ref, keys_ref, grad_ref, value_ref, state_ref):
    width = keys_ref.shape[1]
    count = keys_ref.shape[0] // GROUP
    places = lax.broadcasted_iota(jnp.int32, (count, count), 0)
    others = lax.broadcasted_iota(jnp.int32, (count, count), 1)
    for off in range(GROUP):
        span = slice(off * count, (off + 1) * count)
        rows = all_ref[span, :]
        lifted, values, dout = (split(part(rows, k, width)) for k in range(3))
        keys = split(keys_ref[span, :])
        mixed = jnp.where(others >= places, dot3(keys, lifted, True), 0.0)
        carried = dot3(keys, split(grad_ref[off * width : (off + 1) * width, :]), True)
        value_ref[span, :] = carried + scale * dot3(split(mixed), dout)
        scores = jnp.where(places >= others, dot3(dout, values, True), 0.0)
        state_ref[span, :] = dot3(split(scores), keys)


def results(all_ref, sums_ref, before_ref, state_ref, value_ref, own, near, far, both):
    width = before_ref.shape[1]
    count = state_ref.shape[0] // GROUP
    for off, ref in enumerate((own, near, far, both)):
        span = slice(off * count, (off + 1) * count)
        before = sums_ref[off * width : (off + 1) * width, :] + before_ref[...]
        state = state_ref[span, :] + dot3(split(all_ref[span, 2 * width :]), split(before))
        ref[:, :width] = state.astype(ref.dtype)
        ref[:, width:] = value_ref[span, :].astype(ref.dtype)


def at_home(scale, place_ref, q_ref, routing_ref, gates_ref, own, near, far, both, query_ref, value_ref, gate_ref):
    queries = q_ref[...]
    width = queries.shape[1]
    query = jnp.zeros_like(queries)
    value = jnp.zeros_like(queries)
    gate = jnp.zeros(gate_ref.shape, F32)
    ones = jnp.ones((gate.shape[0], 2 * width), BF16)
    routers = router_columns(place_ref[0], routing_ref[...], gates_ref[...])
    for (weight, routed, hit), ref in zip(routers, (own, near, far, both), strict=True):
        state = ref[:, :width].astype(F32)
        query = query + weight * state
        value = value + routed * ref[:, width:].astype(F32)
        terms = jnp.concatenate(split(queries * state), axis=1)
        mine = lax.dot_general(ones, terms, (((1,), (1,)), ((), ())), preferred_element_type=F32)
        gate = gate + jnp.where(hit, mine, 0.0)
    query_ref[...] = scale * query
    value_ref[...] = value
    gate_ref[...] = scale * gate


def by_column(place_ref, x_ref, own, near, far, both):
    size = own.shape[1]
    for off, ref in enumerate((own, near, far, both)):
        ref[...] = x_ref[:, pl.ds(pl.multiple_of((place_ref[0] ^ off) * size, size), size)]


def by_row(place_ref, *refs):
    parts, (own, near, far, both, room) = refs[:-5], refs[-5:]
    size = own.shape[0]
    total = parts[0][...]
    for ref in parts[1:]:
        total = total + ref[...].astype(F32)
    room[...] = total
    for off, ref in enumerate((own, near, far, both)):
        ref[...] = room[pl.ds(pl.multiple_of((place_ref[0] ^ off) * size, size), size), :]


def in_columns(place_ref, own, near, far, both, out_ref):
    size = own.shape[1]
    for off, ref in enumerate((own, near, far, both)):
        out_ref[:, pl.ds(pl.multiple_of((place_ref[0] ^ off) * size, size), size)] = ref[...]


def swap(x, off, parts):
    return lax.ppermute(x, "ctx", [(i, i ^ off) for i in range(parts)])


def other_core(x):
    return lax.ppermute(x, "head", [(i, i ^ 1) for i in range(lax.axis_size("head"))])


def from_groups(total, steps, parts):
    return [swap(total, off, parts) for off in steps[1:]]


def prefix(total, got, steps, here, reverse):
    before = jnp.zeros_like(total)
    for off, x in zip(steps[1:], got, strict=True):
        other = here ^ off
        before = before + jnp.where(other > here if reverse else other < here, x, 0.0)
    return before


def over_heads(x):
    count = lax.axis_size("head")
    bit = 1
    while bit < count:
        x = x + lax.ppermute(x, "head", [(i, i ^ bit) for i in range(count)])
        bit *= 2
    return x


def on_device(tokens, queries, values, dout, key_weight, routing, gates):
    count, width = tokens.shape
    rows, memories, head_dim = key_weight.shape
    parts = lax.axis_size("ctx")
    steps = list(range(0, parts, GROUP))
    here = lax.axis_index("ctx").astype(jnp.int32)
    core = lax.axis_index("head").astype(jnp.int32) & 1
    at = jnp.stack([here & (GROUP - 1), core, here // GROUP, here])
    scale = 1.0 / math.sqrt(head_dim * count * parts)
    tall = GROUP * count
    smem = pl.BlockSpec(memory_space=pltpu.SMEM)
    vmem = pl.BlockSpec(memory_space=pltpu.VMEM)
    anywhere = pl.BlockSpec(memory_space=pl.ANY)

    def shape(r, c, dtype=F32):
        return jax.ShapeDtypeStruct((r, c), dtype)

    def stack(*blocks, waits=()):
        size = sum(x.shape[0] for x in blocks)
        return call(
            pack,
            shape(size, blocks[0].shape[1], blocks[0].dtype),
            *blocks,
            spaces=[anywhere] * len(blocks),
            scratch=[pltpu.SemaphoreType.DMA((len(blocks),))],
            waits=waits,
        )

    half = lax.dynamic_slice(tokens, (core * (count // 2), jnp.int32(0)), (count // 2, width))
    from_x, from_y = swap(half, 1, parts), swap(half, 2, parts)

    mine = call(
        by_column,
        [shape(rows, head_dim, BF16)] * 4,
        at, key_weight.reshape(rows, memories * head_dim),
        spaces=[smem, vmem],
    )
    weights = [mine[0]] + [swap(mine[off], off, parts) for off in (1, 2, 3)]

    sent = call(
        messages,
        [shape(count, 3 * head_dim)] + [shape(count + TAIL, 3 * head_dim)] * 3,
        at, queries, values, dout, routing.T, gates.T,
        spaces=[smem] + [anywhere] * 5,
        scratch=[pltpu.VMEM((count, head_dim), F32)] * 3
        + [pltpu.VMEM(x.shape[::-1], x.dtype) for x in (routing, gates)]
        + [pltpu.SemaphoreType.DMA((5,))],
    )
    coded = [x.astype(F16) for x in sent[1:]]
    got = [swap(x, off, parts).astype(F32) for off, x in zip((3, 2, 1), coded[::-1])][::-1]

    neighbours = stack(from_x, from_y, waits=(*sent[1:], *weights))
    neighbours_other = other_core(neighbours)

    block = stack(*weights, waits=sent[1:])
    chunks, layout, held = [block], [list(range(GROUP))], list(range(GROUP))
    bit = parts // 2
    while bit >= GROUP:
        other = swap(block, bit, parts)
        chunks.append(other)
        layout.append([off ^ bit for off in held])
        held = held + layout[-1]
        if bit > GROUP:
            block = stack(block, other)
        bit //= 2

    quarter = count // 4
    last_a, last_b = call(
        cut,
        [shape(quarter, width, BF16)] * 2,
        from_x, from_y,
        spaces=[anywhere] * 2,
        scratch=[pltpu.SemaphoreType.DMA((2,))],
        waits=(*got, neighbours_other),
    )
    last_a, last_b = swap(last_a, 2, parts), swap(last_b, 1, parts)

    every, grad_sums, total = call(
        functools.partial(grad_states, scale),
        [shape(tall, 3 * head_dim), shape(GROUP * head_dim, head_dim), shape(head_dim, head_dim)],
        at, sent[0], *got,
        spaces=[smem] + [vmem] * 4,
        waits=(neighbours_other,),
        flops=6 * tall * head_dim * head_dim,
    )
    totals = from_groups(total, steps, parts)
    before = prefix(total, totals, steps, here, True)
    inner_k = call(
        functools.partial(inner_key, scale),
        shape(tall, head_dim),
        every,
        flops=12 * tall * count * head_dim,
    )
    low, grad_in = call(
        key_low,
        [shape(tall, head_dim, BF16), shape(GROUP * head_dim, head_dim)],
        every, grad_sums, before, inner_k,
        flops=6 * tall * head_dim * head_dim,
    )

    first, weights = call(
        functools.partial(first_keys, layout, parts),
        [shape(3 * count, head_dim), shape(width, head_dim, BF16)],
        at, *chunks, tokens, neighbours, neighbours_other,
        spaces=[smem] + [vmem] * (3 + len(chunks)),
        waits=(inner_k,),
        flops=2 * tall * width * head_dim,
    )
    product, last_low = call(
        first_products,
        [shape(head_dim, width), shape(head_dim, count, BF16)],
        at, tokens, neighbours, neighbours_other, low,
        spaces=[smem] + [vmem] * 4,
        scratch=[pltpu.VMEM((tall, head_dim), BF16)],
        flops=2 * tall * width * head_dim,
    )
    last = stack(last_a, last_b, waits=(first[:8], *totals))
    last_other = other_core(last)

    keys, sums, key_total = call(
        key_states,
        [shape(tall, head_dim), shape(GROUP * head_dim, head_dim), shape(head_dim, head_dim)],
        at, first, weights, last, last_other, every,
        spaces=[smem] + [vmem] * 5,
        flops=2 * count * width * head_dim,
    )
    key_totals = from_groups(key_total, steps, parts)

    span = width // len(steps)
    sent = call(
        functools.partial(products, steps),
        [shape(span, head_dim)] + [shape(span, head_dim, BF16)] * (len(steps) - 1),
        at, product, last_low, last, last_other,
        spaces=[smem] + [vmem] * 4,
        waits=(key_total,),
        scratch=[pltpu.VMEM((head_dim, width), F32)],
        flops=2 * count * width * head_dim,
    )
    parts_of_sum = [sent[0]] + [swap(x, off, parts) for off, x in zip(steps[1:], sent[1:], strict=True)]
    inner_v, inner_state = call(
        functools.partial(inner_rest, scale),
        [shape(tall, head_dim)] * 2,
        every, keys, grad_in,
        waits=(sent[0],),
        flops=24 * tall * count * head_dim,
    )

    mine = call(
        by_row,
        [shape(rows, head_dim)] * 4,
        at, *parts_of_sum,
        spaces=[smem] + [vmem] * len(steps),
        scratch=[pltpu.VMEM((GROUP * rows, head_dim), F32)],
    )
    others = [swap(mine[off], off, parts) for off in (1, 2, 3)]

    before = prefix(key_total, key_totals, steps, here, False)
    sent = call(
        results,
        [shape(count, 2 * head_dim)] + [shape(count, 2 * head_dim, BF16)] * 3,
        every, sums, before, inner_state, inner_v,
        flops=6 * tall * head_dim * head_dim,
    )
    query_grad, value_grad, gate_part = call(
        functools.partial(at_home, scale),
        [shape(count, head_dim), shape(count, head_dim), shape(routing.shape[1], count)],
        at, queries, routing.T, gates.T, sent[0], *[swap(sent[off], off, parts) for off in (3, 2, 1)][::-1],
        spaces=[smem] + [vmem] * 7,
        waits=mine,
    )
    gate_grad = over_heads(gate_part).T
    key_grad = call(
        in_columns,
        shape(rows, memories * head_dim),
        at, mine[0], *others,
        spaces=[smem] + [vmem] * 4,
    ).reshape(rows, memories, head_dim)
    return (key_grad, query_grad, value_grad, gate_grad)


def solution(mesh):
    return jax.shard_map(
        on_device,
        mesh=mesh,
        in_specs=(
            P("ctx", None),
            P("ctx", "head"),
            P("ctx", "head"),
            P("ctx", "head"),
            P("ctx", None, "head"),
            P("ctx", None),
            P("ctx", None),
        ),
        out_specs=(P("ctx", None, "head"), P("ctx", "head"), P("ctx", "head"), P("ctx", None)),
        check_vma=False,
    )
```
